256 devices in a mesh: fsdp: 64 (over x, z, core), mp: 4 (over y).
Axes of the slice: x: 4, y: 4, z: 8, core: 2. Of those that a mesh axis runs over, the one named last changes fastest.
Arguments:
- gradient: bfloat16 [4096, 14336], P('fsdp', 'mp')
- first_moment: float32 [4096, 14336], P('fsdp', 'mp'), may hold values from -4 to 4
- left_gram: float32 [64, 4, 512, 512], P('fsdp', 'mp')
- right_gram: float32 [64, 4, 512, 512], P('fsdp', 'mp')
- left_basis: bfloat16 [64, 4, 512, 512], P('fsdp', 'mp'), may hold values from -0.25 to 0.25
- right_basis: bfloat16 [64, 4, 512, 512], P('fsdp', 'mp'), may hold values from -0.25 to 0.25
- second_moment: float32 [64, 4, 512, 512], P('fsdp', 'mp'), may hold values from 0.02 to 0.2
- block_target: int32 [4, 56], P('mp'), may hold values from 0 to 63, as said below
Outputs:
- param_update: bfloat16 [4096, 14336], P('fsdp', 'mp')
- first_next: float32 [4096, 14336], P('fsdp', 'mp')
- left_next: float32 [64, 4, 512, 512], P('fsdp', 'mp')
- right_next: float32 [64, 4, 512, 512], P('fsdp', 'mp')
- second_next: float32 [64, 4, 512, 512], P('fsdp', 'mp')
The draws below stay inside these ranges and needn't reach their ends.
Inputs may be any that keep to these rules, and one draw needn't show every extreme that they name: `block_target`: A value names the fsdp owner of a block. Values within one row are distinct.
All inputs are finite; a program needn't handle non-finite values.
Results may differ from the reference program's by a relative error of at most 0.0061.
Values may be sent and summed in bfloat16 or wider, within the bound.
A program may use at most 64 MiB of HBM per device.

```python
import math
import jax
import jax.numpy as jnp
from jax import lax

BLOCK = 512
FFN = 14336
ROWS = 4096
BANDS = 8
COLBLK = 7
BLOCKS = 56
N_FSDP = 64
N_MP = 4


def gram_field(key, spread):
    noise_key, diag_key = jax.random.split(key)
    shape = (N_FSDP, N_MP, BLOCK, BLOCK)
    noise = jax.random.normal(noise_key, shape, jnp.float32) * spread
    symmetric = noise + jnp.swapaxes(noise, 2, 3)
    diagonal = jnp.exp(jax.random.uniform(diag_key, shape[:3], jnp.float32, math.log(0.02), math.log(0.2)))
    identity = (jnp.arange(BLOCK)[:, None] == jnp.arange(BLOCK)[None, :]).astype(jnp.float32)
    return symmetric + identity * diagonal[..., None]


def draw_left_gram(key, part):
    key = jax.random.fold_in(key, 3)
    return gram_field(key, 0.004)


def draw_right_gram(key, part):
    key = jax.random.fold_in(key, 5)
    return gram_field(key, 0.004)


def group_scales(key):
    order = jax.random.permutation(key, N_MP).astype(jnp.float32)
    level = order / float(max(N_MP - 1, 1))
    group_factor = jnp.exp(math.log(10.0) * (-0.75 + 1.5 * level))
    column_group = jnp.arange(FFN, dtype=jnp.int32) // (FFN // N_MP)
    return group_factor[column_group][None, :]


def draw_gradient(key, part):
    key = jax.random.fold_in(key, 11)
    base_key = jax.random.fold_in(key, 0)
    row_key = jax.random.fold_in(key, 1)
    col_key = jax.random.fold_in(key, 2)
    group_key = jax.random.fold_in(key, 4)
    position = jnp.arange(ROWS, dtype=jnp.float32) / (ROWS - 1)
    row_factor = jnp.exp(jax.random.uniform(row_key, (ROWS, 1), jnp.float32) * math.log(10.0))
    col_factor = jnp.exp(jax.random.uniform(col_key, (1, FFN), jnp.float32) * math.log(10.0))
    group_factor = group_scales(group_key)
    rising = 1.0 + 2.0 * position
    values = jax.random.normal(base_key, (ROWS, FFN), jnp.float32)
    return (values * rising[:, None] * row_factor * col_factor * group_factor).astype(jnp.bfloat16)


def draw_block_target(key, part):
    key = jax.random.fold_in(key, 7)

    def one_group(group):
        group_key = jax.random.fold_in(key, group)
        perm_key, order_key = jax.random.split(group_key)
        owners = jax.random.permutation(perm_key, N_FSDP)
        first_owner = owners[0]
        owners = jnp.where(owners == N_FSDP - 1, first_owner, owners)
        owners = owners.at[0].set(N_FSDP - 1)
        band_keys = jax.random.split(order_key, BANDS)
        column_order = jax.vmap(lambda band_key: jax.random.permutation(band_key, COLBLK))(band_keys)
        position = (jnp.arange(BANDS)[:, None] * COLBLK + column_order).reshape(BLOCKS)
        return owners[position].astype(jnp.int32)
    return jax.vmap(one_group)(jnp.arange(N_MP))


def block_levels(key, dims, cuts, least, largest):
    def one(dim, parts):
        draws = jax.random.uniform(jax.random.fold_in(jax.random.fold_in(key, 6), dim), (parts,), jnp.float32, least / len(cuts), largest / len(cuts))
        return jnp.repeat(jnp.exp(draws), dims[dim] // parts).reshape((-1,) + (1,) * (len(dims) - dim - 1))

    factor_of = one(*cuts[0])
    for cut in cuts[1:]:
        factor_of = factor_of * one(*cut)
    return factor_of


def bell_draw(rng, dims, width, limit, shards=(), held_as=jnp.bfloat16):
    result = width * jax.random.normal(rng, dims, jnp.float32)
    if shards:
        result = result * block_levels(rng, dims, shards, -0.22, 0.18)
    return jnp.clip(result, -limit, limit).astype(held_as)


def setup_inputs(seed: int = 0) -> dict:
    splits = jax.random.split(jax.random.key(seed), 9)
    return {
        "gradient": draw_gradient(jax.random.fold_in(splits[8], 71), 0),
        "first_moment": bell_draw(splits[1], (ROWS, FFN), 0.3, 4.0, ((0, 64), (1, 4)), jnp.float32),
        "left_gram": draw_left_gram(jax.random.fold_in(splits[8], 71), 0),
        "right_gram": draw_right_gram(jax.random.fold_in(splits[8], 71), 0),
        "left_basis": bell_draw(splits[4], (N_FSDP, N_MP, BLOCK, BLOCK), BLOCK ** -0.5, 0.25, ((0, 64), (1, 4))),
        "right_basis": bell_draw(splits[5], (N_FSDP, N_MP, BLOCK, BLOCK), BLOCK ** -0.5, 0.25, ((0, 64), (1, 4))),
        "second_moment": jnp.clip(jnp.exp(math.log(0.2) - 2.3025851 * jax.random.uniform(splits[6], (N_FSDP, N_MP, BLOCK, BLOCK), jnp.float32) ** block_levels(splits[6], (N_FSDP, N_MP, BLOCK, BLOCK), ((0, 64), (1, 4)), -0.2, 0.2)), 0.02, 0.2),
        "block_target": draw_block_target(jax.random.fold_in(splits[8], 71), 0),
    }


CLIP_RMS = 0.5
FIRST_DECAY = 0.9
GRAM_DECAY = 0.95
GRAM_RATE = 0.05
SECOND_DECAY = 0.95
SECOND_RATE = 0.05
EPSILON = 1e-08

def reference(gradient, first_moment, left_gram, right_gram, left_basis, right_basis, second_moment, block_target):
    grad_wide = gradient.astype(jnp.float32)
    norm_sum = jnp.sum(grad_wide * grad_wide)
    clip_factor = jnp.minimum(1.0, CLIP_RMS * jnp.sqrt(float(ROWS * FFN)) / jnp.sqrt(norm_sum))
    first_next = FIRST_DECAY * first_moment + (1.0 - FIRST_DECAY) * clip_factor * grad_wide
    moment = first_next.astype(jnp.bfloat16)
    group_cols = FFN // N_MP

    def block_step(carry, index):
        param_update, left_next, right_next, second_next = carry
        group = index // BLOCKS
        within = index % BLOCKS
        row_start = (within // COLBLK * BLOCK).astype(jnp.int32)
        col_start = (group * group_cols + within % COLBLK * BLOCK).astype(jnp.int32)
        grad_block = lax.dynamic_slice(gradient, (row_start, col_start), (BLOCK, BLOCK))
        moment_block = lax.dynamic_slice(moment, (row_start, col_start), (BLOCK, BLOCK))
        target_slot = block_target[group, within]
        left_mat = left_basis[target_slot, group]
        right_mat = right_basis[target_slot, group]
        gram_scale = GRAM_RATE * clip_factor * clip_factor / BLOCK
        gram_left = jnp.dot(grad_block, grad_block.T, preferred_element_type=jnp.float32)
        gram_right = jnp.dot(grad_block.T, grad_block, preferred_element_type=jnp.float32)
        left_new = GRAM_DECAY * left_gram[target_slot, group] + gram_scale * gram_left
        right_new = GRAM_DECAY * right_gram[target_slot, group] + gram_scale * gram_right
        left_half = jnp.dot(left_mat.T, grad_block, preferred_element_type=jnp.float32).astype(jnp.bfloat16)
        rotated = clip_factor * jnp.dot(left_half, right_mat, preferred_element_type=jnp.float32)
        second_new = SECOND_DECAY * second_moment[target_slot, group] + SECOND_RATE * rotated * rotated
        moment_half = jnp.dot(left_mat.T, moment_block, preferred_element_type=jnp.float32).astype(jnp.bfloat16)
        moment_rot = jnp.dot(moment_half, right_mat, preferred_element_type=jnp.float32)
        normed = (moment_rot / (jnp.sqrt(second_new) + EPSILON)).astype(jnp.bfloat16)
        back_half = jnp.dot(left_mat, normed, preferred_element_type=jnp.float32).astype(jnp.bfloat16)
        slot_update = jnp.dot(back_half, right_mat.T, preferred_element_type=jnp.float32).astype(jnp.bfloat16)
        param_update = lax.dynamic_update_slice(param_update, slot_update, (row_start, col_start))
        left_next = left_next.at[target_slot, group].set(left_new)
        right_next = right_next.at[target_slot, group].set(right_new)
        second_next = second_next.at[target_slot, group].set(second_new)
        return ((param_update, left_next, right_next, second_next), None)
    start = (jnp.zeros((ROWS, FFN), jnp.bfloat16), left_gram, right_gram, second_moment)
    finish, _ = lax.scan(block_step, start, jnp.arange(N_MP * BLOCKS, dtype=jnp.int32))
    param_update, left_next, right_next, second_next = finish
    return (param_update, first_next, left_next, right_next, second_next)
```

```python
import functools

import jax
import jax.numpy as jnp
from jax import lax
from jax.experimental import pallas as pl
from jax.experimental.pallas import tpu as pltpu
from jax.sharding import PartitionSpec as P

CLIP_RMS = 0.5
FIRST_DECAY = 0.9
GRAM_DECAY = 0.95
GRAM_RATE = 0.05
SECOND_DECAY = 0.95
SECOND_RATE = 0.05
EPSILON = 1e-08

MESH = pl.DeviceIdType.MESH
NX, NZ, NC = 4, 8, 2
HALF = NZ // 2
COLBLK = 7
SLOTS = NX * NC
LOCAL = NX * COLBLK
ROWS = 64
BLOCK = 512
LANE = BLOCK // NX
CHUNKS = 2
RC = ROWS // CHUNKS
Z_ORDER = (4, 5, 3, 6, 2, 7, 1)
X_ORDER = (2, 1, 3)

BF16, F32 = jnp.bfloat16, jnp.float32


def mm(a, b):
    return jnp.dot(a, b, preferred_element_type=F32)


def kernel(
    n_entries,
    tgt_hbm,
    grad_hbm,
    first_hbm,
    lg_hbm,
    rg_hbm,
    ql_hbm,
    qr_hbm,
    sm_hbm,
    upd_hbm,
    fn_hbm,
    ln_hbm,
    rn_hbm,
    sn_hbm,
    g_v,
    f_v,
    lg_v,
    rg_v,
    ql_v,
    qr_v,
    sm_v,
    out_v,
    qlt_v,
    qrt_v,
    den_v,
    norm_s,
    norm_z,
    norm_x,
    norm_y,
    xs,
    xr,
    zs,
    zr_,
    gs,
    gr,
    blk,
    ub,
    ug,
    uz,
    us,
    uf,
    tgt_s,
    tgt_v,
    tbl_v,
    tbl,
    in_sem,
    out_sem,
    nsend,
    nrecv,
    xsend,
    xrecv,
    zsend,
    zrecv,
    gsend,
    grecv,
):
    f = lax.axis_index("fsdp")
    q = lax.axis_index("mp")
    tgt_loads = [
        pltpu.make_async_copy(tgt_hbm, tgt_s, in_sem.at[7]),
        pltpu.make_async_copy(tgt_hbm, tgt_v, in_sem.at[8]),
    ]
    for load in tgt_loads:
        load.start()
    c = lax.rem(f, NC)
    z = lax.rem(f // NC, NZ)
    x = f // (NC * NZ)
    n_mp = lax.axis_size("mp")

    def fid(xx, zz, cc):
        return (xx * NZ + zz) * NC + cc

    def rot(v, d, n):
        return lax.rem(v + d, n)

    loads = [
        pltpu.make_async_copy(src, dst, in_sem.at[i])
        for i, (src, dst) in enumerate(
            (
                (grad_hbm, g_v),
                (first_hbm, f_v),
                (ql_hbm, ql_v),
                (qr_hbm, qr_v),
                (sm_hbm, sm_v),
                (lg_hbm, lg_v),
                (rg_hbm, rg_v),
            )
        )
    ]
    for load in loads:
        load.start()

    barrier = pltpu.get_barrier_semaphore()
    peers = [(fid(x, rot(z, d, NZ), c), q) for d in Z_ORDER]
    peers += [
        (fid(rot(x, dx, NX), z, rot(c, dc, NC)), q)
        for dx in range(NX)
        for dc in range(NC)
        if dx or dc
    ]
    peers += [(f, rot(q, d, n_mp)) for d in range(1, n_mp)]
    for pf, pq in peers:
        pl.semaphore_signal(barrier, inc=1, device_id=(pf, pq), device_id_type=MESH)
    pl.semaphore_wait(barrier, len(peers))

    def send(src, dst, ssem, rsem, pf, pq):
        pltpu.make_async_remote_copy(
            src_ref=src,
            dst_ref=dst,
            send_sem=ssem,
            recv_sem=rsem,
            device_id=(pf, pq),
            device_id_type=MESH,
        ).start()

    def wait_bytes(ref, sem):
        pltpu.make_async_copy(ref, ref, sem).wait()

    def spread_stage(a, r, rows):
        for xx in range(NX):
            for j in range(COLBLK):
                lo = j * BLOCK + xx * LANE
                xs[a, r, xx, j] = rows[:, lo : lo + LANE]

    def spread_send(a, r):
        for d in X_ORDER:
            px = rot(x, d, NX)
            send(
                xs.at[a, r, px], xr[a][r].at[x], xsend.at[a, r], xrecv.at[a, r], fid(px, z, c), q
            )
        xr[a][r][x] = xs[a, r, x]

    def z_stage(a, r):
        wait_bytes(xr[a][r].at[pl.ds(0, NX - 1)], xrecv.at[a, r])

        def slots(pz, dst):
            for s in range(SLOTS):
                owner = fid(s // NC, pz, s % NC)
                l = tbl[0, owner]
                dst[s] = xr[a][r][l // COLBLK, lax.rem(l, COLBLK)]

        for d in Z_ORDER:
            pz = rot(z, d, NZ)
            slots(pz, zs.at[a, r, pz])
            send(
                zs.at[a, r, pz], zr_[a][r].at[z], zsend.at[a, r], zrecv.at[a, r], fid(x, pz, c), q
            )
        slots(z, zr_[a][r].at[z])

    def gather_stage(a, r):
        wait_bytes(zr_[a][r].at[pl.ds(0, NZ - 1)], zrecv.at[a, r])
        for s in range(SLOTS):
            h = tbl[1, fid(s // NC, z, s % NC)]
            for i in range(HALF):
                gs[a, r, s, i] = zr_[a][r][h * HALF + i, s]
        for dx in X_ORDER + (0,):
            for dc in range(NC):
                if dx or dc:
                    px, pc = rot(x, dx, NX), rot(c, dc, NC)
                    send(
                        gs.at[a, r, px * NC + pc],
                        gr.at[a, r, x, c],
                        gsend.at[a, r],
                        grecv.at[a, r],
                        fid(px, z, pc),
                        q,
                    )
        gr[a, r, x, c] = gs[a, r, x * NC + c]

    def assemble(a, r):
        wait_bytes(gs.at[a, r, pl.ds(0, SLOTS - 1)], grecv.at[a, r])
        for xx in range(NX):
            for cc in range(NC):
                for i in range(HALF):
                    blk[a, i * NC + cc, r * RC : (r + 1) * RC, xx * LANE : (xx + 1) * LANE] = gr[
                        a, r, xx, cc, i
                    ]

    loads[0].wait()
    for r in range(CHUNKS):
        spread_stage(0, r, g_v[r * RC : (r + 1) * RC, :])
        spread_send(0, r)

    for load in tgt_loads:
        load.wait()
    n_blocks = tgt_v.shape[1]
    sub = lax.broadcasted_iota(jnp.int32, (n_blocks, 128), 0)
    lane = lax.broadcasted_iota(jnp.int32, (n_blocks, 128), 1)
    sub_sq = lax.broadcasted_iota(jnp.int32, (n_blocks, n_blocks), 0)
    lane_sq = lax.broadcasted_iota(jnp.int32, (n_blocks, n_blocks), 1)
    diag = jnp.where(sub_sq == lane_sq, jnp.broadcast_to(tgt_v[...], sub_sq.shape), 0)
    named = jnp.sum(diag, axis=1, keepdims=True) == lane
    band = sub // COLBLK
    side = lax.rem(band, 2)
    local = jnp.where(side == z // HALF, sub - (band - band // 2) * COLBLK, 0)
    for i, code in enumerate((local, side, jnp.ones_like(sub))):
        tbl_v[i : i + 1, :] = jnp.max(jnp.where(named, code, 0), axis=0, keepdims=True)
    tbl_copy = pltpu.make_async_copy(tbl_v, tbl, in_sem.at[9])
    tbl_copy.start()

    wide = g_v[...].astype(F32)
    cols = jnp.sum((wide * wide).reshape(ROWS // 8, 8, wide.shape[1]), axis=0)
    acc = cols[:, :128]
    for i in range(1, cols.shape[1] // 128):
        acc = acc + cols[:, i * 128 : (i + 1) * 128]
    norm_s[0] = acc
    norm_z[z] = acc
    for d in Z_ORDER:
        send(norm_s.at[0], norm_z.at[z], nsend.at[0], nrecv.at[0], fid(x, rot(z, d, NZ), c), q)

    tbl_copy.wait()
    z_stage(0, 0)

    wait_bytes(norm_z.at[pl.ds(0, NZ - 1)], nrecv.at[0])
    acc = jnp.sum(norm_z[...], axis=0)
    norm_s[1] = acc
    norm_x[x] = acc
    for d in X_ORDER:
        send(norm_s.at[1], norm_x.at[x], nsend.at[1], nrecv.at[1], fid(rot(x, d, NX), z, c), q)

    for r in range(1, CHUNKS):
        z_stage(0, r)

    wait_bytes(norm_x.at[pl.ds(0, NX - 1)], nrecv.at[1])
    acc = jnp.sum(norm_x[...], axis=0)
    norm_s[2] = acc
    norm_y[q] = acc
    for d in range(1, n_mp):
        send(norm_s.at[2], norm_y.at[q], nsend.at[2], nrecv.at[2], f, rot(q, d, n_mp))
    wait_bytes(norm_y.at[pl.ds(0, n_mp - 1)], nrecv.at[2])
    acc = jnp.sum(norm_y[...], axis=0)
    norm_s[3] = acc
    norm_s[4] = acc
    send(norm_s.at[3], norm_s.at[5], nsend.at[3], nrecv.at[3], fid(x, z, 1 - c), q)
    wait_bytes(norm_s.at[5], nrecv.at[3])
    acc = norm_s[4] + norm_s[5]
    norm_sum = jnp.sum(jnp.sum(acc, axis=0, keepdims=True), axis=1, keepdims=True)
    clip = jnp.minimum(1.0, CLIP_RMS * (float(n_entries) ** 0.5) / jnp.sqrt(norm_sum))

    loads[1].wait()
    for r in range(CHUNKS):
        rows = slice(r * RC, (r + 1) * RC)
        nxt = FIRST_DECAY * f_v[rows, :] + ((1.0 - FIRST_DECAY) * clip) * g_v[rows, :].astype(F32)
        f_v[rows, :] = nxt
        spread_stage(1, r, nxt.astype(BF16))
        spread_send(1, r)
    stores = [pltpu.make_async_copy(f_v, fn_hbm, out_sem.at[0])]
    stores[0].start()
    for r in range(CHUNKS):
        z_stage(1, r)

    for load in loads[2:]:
        load.wait()
    left = ql_v[...].reshape(BLOCK, BLOCK)
    qlt_v[...] = left.T
    qrt_v[...] = qr_v[...].T
    for r in range(CHUNKS):
        gather_stage(0, r)
    for r in range(CHUNKS):
        assemble(0, r)
    live = tbl[2, f] > 0
    block = blk[0].reshape(BLOCK, BLOCK)
    half = mm(qlt_v[...], block).astype(BF16)
    rotated = clip * mm(half, qr_v[...])
    second = SECOND_DECAY * sm_v[...] + SECOND_RATE * rotated * rotated
    den_v[...] = jnp.sqrt(second) + EPSILON
    sm_v[...] = jnp.where(live, second, sm_v[...])
    stores.append(pltpu.make_async_copy(sm_v, sn_hbm, out_sem.at[1]))
    stores[-1].start()
    scale = GRAM_RATE * clip * clip / BLOCK
    block_t = block.T
    lg_v[...] = jnp.where(live, GRAM_DECAY * lg_v[...] + scale * mm(block, block_t), lg_v[...])
    stores.append(pltpu.make_async_copy(lg_v, ln_hbm, out_sem.at[2]))
    stores[-1].start()
    rg_v[...] = jnp.where(live, GRAM_DECAY * rg_v[...] + scale * mm(block_t, block), rg_v[...])
    stores.append(pltpu.make_async_copy(rg_v, rn_hbm, out_sem.at[3]))
    stores[-1].start()

    for r in range(CHUNKS):
        gather_stage(1, r)
    for r in range(CHUNKS):
        assemble(1, r)
    mhalf = mm(qlt_v[...], blk[1].reshape(BLOCK, BLOCK)).astype(BF16)
    normed = (mm(mhalf, qr_v[...]) / den_v[...]).astype(BF16)
    me = x * NC + c
    for r in range(CHUNKS):
        rows = ql_v[:, r * RC : (r + 1) * RC, :].reshape(HALF * NC * RC, BLOCK)
        upd = mm(mm(rows, normed).astype(BF16), qrt_v[...]).astype(BF16)
        for xx in range(NX):
            for cc in range(NC):
                for i in range(HALF):
                    lo = (i * NC + cc) * RC
                    ub[r, xx, cc, i] = upd[lo : lo + RC, xx * LANE : (xx + 1) * LANE]
        for dx in X_ORDER + (0,):
            for dc in range(NC):
                if dx or dc:
                    px, pc = rot(x, dx, NX), rot(c, dc, NC)
                    send(
                        ub.at[r, px, pc],
                        ug.at[r, me],
                        gsend.at[2, r],
                        grecv.at[2, r],
                        fid(px, z, pc),
                        q,
                    )
        ug[r, me] = ub[r, x, c]

    for r in range(CHUNKS):
        wait_bytes(ug.at[r, pl.ds(0, SLOTS - 1)], grecv.at[2, r])
        for d in Z_ORDER:
            pz = rot(z, d, NZ)
            send(
                ug.at[r, :, lax.rem(pz, HALF)],
                uz[r].at[z],
                zsend.at[2, r],
                zrecv.at[2, r],
                fid(x, pz, c),
                q,
            )
        for s in range(SLOTS):
            uz[r][z, s] = ug[r, s, lax.rem(z, HALF)]
    for r in range(CHUNKS):
        wait_bytes(uz[r].at[pl.ds(0, NZ - 1)], zrecv.at[2, r])
        for xx in range(NX):
            for j in range(COLBLK):
                t = tgt_s[0, (xx * 2 + z // HALF) * COLBLK + j]
                slot = (t // (NC * NZ)) * NC + lax.rem(t, NC)
                us[r, xx, j] = uz[r][lax.rem(t // NC, NZ), slot]
        for d in X_ORDER:
            px = rot(x, d, NX)
            send(us.at[r, px], uf.at[r, x], xsend.at[2, r], xrecv.at[2, r], fid(px, z, c), q)
        uf[r, x] = us[r, x]
    for r in range(CHUNKS):
        wait_bytes(uf.at[r, pl.ds(0, NX - 1)], xrecv.at[2, r])
        for xx in range(NX):
            for j in range(COLBLK):
                lo = j * BLOCK + xx * LANE
                out_v[r * RC : (r + 1) * RC, lo : lo + LANE] = uf[r, xx, j]
    stores.append(pltpu.make_async_copy(out_v, upd_hbm, out_sem.at[4]))
    stores[-1].start()

    wait_bytes(norm_z.at[pl.ds(0, NZ - 1)], nsend.at[0])
    wait_bytes(norm_x.at[pl.ds(0, NX - 1)], nsend.at[1])
    wait_bytes(norm_y.at[pl.ds(0, n_mp - 1)], nsend.at[2])
    wait_bytes(norm_s.at[3], nsend.at[3])
    for r in range(CHUNKS):
        for a in range(2):
            wait_bytes(xs.at[a, r, pl.ds(0, NX - 1)], xsend.at[a, r])
            wait_bytes(zs.at[a, r, pl.ds(0, NZ - 1)], zsend.at[a, r])
            wait_bytes(gs.at[a, r, pl.ds(0, SLOTS - 1)], gsend.at[a, r])
        wait_bytes(ug.at[r, pl.ds(0, SLOTS - 1)], gsend.at[2, r])
        wait_bytes(uz[r].at[pl.ds(0, NZ - 1)], zsend.at[2, r])
        wait_bytes(us.at[r, pl.ds(0, NX - 1)], xsend.at[2, r])
    for store in stores:
        store.wait()


def shards(
    gradient,
    first_moment,
    left_gram,
    right_gram,
    left_basis,
    right_basis,
    second_moment,
    block_target,
):
    rows, cols = gradient.shape
    n_fsdp = lax.axis_size("fsdp")
    n_mp = lax.axis_size("mp")
    n_blocks = block_target.shape[1]
    any_spec = pl.BlockSpec(memory_space=pl.ANY)
    vm = pltpu.VMEM
    dma = pltpu.SemaphoreType.DMA
    mat = (BLOCK, BLOCK)
    out = pl.pallas_call(
        functools.partial(kernel, rows * cols * n_fsdp * n_mp),
        out_shape=(
            jax.ShapeDtypeStruct((rows, cols), BF16),
            jax.ShapeDtypeStruct((rows, cols), F32),
            jax.ShapeDtypeStruct(mat, F32),
            jax.ShapeDtypeStruct(mat, F32),
            jax.ShapeDtypeStruct(mat, F32),
        ),
        in_specs=[any_spec] * 8,
        out_specs=(any_spec,) * 5,
        scratch_shapes=[
            vm((rows, cols), BF16),
            vm((rows, cols), F32),
            vm(mat, F32),
            vm(mat, F32),
            vm((HALF * NC, ROWS, BLOCK), BF16),
            vm(mat, BF16),
            vm(mat, F32),
            vm((rows, cols), BF16),
            vm(mat, BF16),
            vm(mat, BF16),
            vm(mat, F32),
            vm((6, 8, 128), F32),
            vm((NZ, 8, 128), F32),
            vm((NX, 8, 128), F32),
            vm((n_mp, 8, 128), F32),
            vm((2, CHUNKS, NX, COLBLK, RC, LANE), BF16),
            [[vm((NX, COLBLK, RC, LANE), BF16)] * CHUNKS] * 2,
            vm((2, CHUNKS, NZ, SLOTS, RC, LANE), BF16),
            [[vm((NZ, SLOTS, RC, LANE), BF16)] * CHUNKS] * 2,
            vm((2, CHUNKS, SLOTS, HALF, RC, LANE), BF16),
            vm((2, CHUNKS, NX, NC, HALF, RC, LANE), BF16),
            vm((2, HALF * NC, ROWS, BLOCK), BF16),
            vm((CHUNKS, NX, NC, HALF, RC, LANE), BF16),
            vm((CHUNKS, SLOTS, HALF, RC, LANE), BF16),
            [vm((NZ, SLOTS, RC, LANE), BF16)] * CHUNKS,
            vm((CHUNKS, NX, COLBLK, RC, LANE), BF16),
            vm((CHUNKS, NX, COLBLK, RC, LANE), BF16),
            pltpu.SMEM((1, n_blocks), jnp.int32),
            vm((1, n_blocks), jnp.int32),
            vm((8, 128), jnp.int32),
            pltpu.SMEM((8, 128), jnp.int32),
            dma((10,)),
            dma((5,)),
            dma((4,)),
            dma((4,)),
            dma((3, CHUNKS)),
            dma((3, CHUNKS)),
            dma((3, CHUNKS)),
            dma((3, CHUNKS)),
            dma((3, CHUNKS)),
            dma((3, CHUNKS)),
        ],
        compiler_params=pltpu.CompilerParams(
            collective_id=0, has_side_effects=True, vmem_limit_bytes=60 * 2**20
        ),
        cost_estimate=pl.CostEstimate(
            flops=16 * BLOCK**3, bytes_accessed=12 * 2**20, transcendentals=BLOCK**2
        ),
    )(
        block_target,
        gradient,
        first_moment,
        left_gram[0, 0],
        right_gram[0, 0],
        left_basis[0, 0].reshape(HALF * NC, ROWS, BLOCK),
        right_basis[0, 0],
        second_moment[0, 0],
    )
    return (out[0], out[1]) + tuple(o[None, None] for o in out[2:])


def solution(mesh):
    return jax.shard_map(
        shards,
        mesh=mesh,
        in_specs=(
            P("fsdp", "mp"),
            P("fsdp", "mp"),
            P("fsdp", "mp", None, None),
            P("fsdp", "mp", None, None),
            P("fsdp", "mp", None, None),
            P("fsdp", "mp", None, None),
            P("fsdp", "mp", None, None),
            P("mp", None),
        ),
        out_specs=(
            P("fsdp", "mp"),
            P("fsdp", "mp"),
            P("fsdp", "mp", None, None),
            P("fsdp", "mp", None, None),
            P("fsdp", "mp", None, None),
        ),
        check_vma=False,
    )
```

```python
import functools

import jax
import jax.numpy as jnp
from jax import lax
from jax.experimental import pallas as pl
from jax.experimental.pallas import tpu as pltpu
from jax.sharding import PartitionSpec as P

CLIP_RMS = 0.5
FIRST_DECAY = 0.9
GRAM_DECAY = 0.95
GRAM_RATE = 0.05
SECOND_DECAY = 0.95
SECOND_RATE = 0.05
EPSILON = 1e-08

MESH = pl.DeviceIdType.MESH
NX, NZ, NC = 4, 8, 2
HALF = NZ // 2
COLBLK = 7
SLOTS = NX * NC
LOCAL = NX * COLBLK
ROWS = 64
BLOCK = 512
LANE = BLOCK // NX
CHUNKS = 4
DIRECT = 2
RC = ROWS // CHUNKS
Z_ORDER = (4, 5, 3, 6, 2, 7, 1)
X_ORDER = (2, 1, 3)

BF16, F32 = jnp.bfloat16, jnp.float32


def mm(a, b):
    return jnp.dot(a, b, preferred_element_type=F32)


def kernel(
    n_entries,
    tgt_hbm,
    grad_hbm,
    first_hbm,
    lg_hbm,
    rg_hbm,
    ql_hbm,
    qr_hbm,
    sm_hbm,
    out_v,
    f_v,
    lg_v,
    rg_v,
    sm_v,
    g_v,
    ql_v,
    qr_v,
    qlt_v,
    qrt_v,
    den_v,
    norm_s,
    norm_y,
    norm_x,
    norm_z,
    xs,
    xr,
    zs,
    zr,
    gs,
    gr,
    blk,
    ms,
    mx,
    mzs,
    mz,
    uds,
    udz,
    udp,
    udx,
    ub,
    ug,
    uz,
    us,
    uf,
    tgt_s,
    tgt_v,
    tbl_v,
    tbl,
    in_sem,
    nsend,
    nrecv,
    xsend,
    xrecv,
    zsend,
    zrecv,
    gsend,
    grecv,
):
    f = lax.axis_index("fsdp")
    q = lax.axis_index("mp")
    c = lax.rem(f, NC)
    z = lax.rem(f // NC, NZ)
    x = f // (NC * NZ)
    side_here = z // HALF
    n_mp = lax.axis_size("mp")

    def fid(xx, zz, cc):
        return (xx * NZ + zz) * NC + cc

    def rot(v, d, n):
        return lax.rem(v + d, n)

    tgt_loads = [
        pltpu.make_async_copy(tgt_hbm, tgt_s, in_sem.at[7]),
        pltpu.make_async_copy(tgt_hbm, tgt_v, in_sem.at[8]),
    ]
    loads = [
        pltpu.make_async_copy(src, dst, in_sem.at[i])
        for i, (src, dst) in enumerate(
            (
                (grad_hbm, g_v),
                (first_hbm, f_v),
                (ql_hbm, ql_v),
                (qr_hbm, qr_v),
                (sm_hbm, sm_v),
                (lg_hbm, lg_v),
                (rg_hbm, rg_v),
            )
        )
    ]
    for load in loads[:1] + tgt_loads + loads[1:]:
        load.start()

    near = [(dx, dc) for dx in X_ORDER + (0,) for dc in range(NC) if dx or dc]
    barrier = pltpu.get_barrier_semaphore()
    peers = [(fid(x, rot(z, d, NZ), rot(c, dc, NC)), q) for d in Z_ORDER for dc in range(NC)]
    peers += [(fid(rot(x, dx, NX), z, rot(c, dc, NC)), q) for dx, dc in near]
    peers += [(f, rot(q, d, n_mp)) for d in range(1, n_mp)]
    for peer in peers:
        pl.semaphore_signal(barrier, inc=1, device_id=peer, device_id_type=MESH)

    for load in tgt_loads:
        load.wait()
    n_blocks = tgt_v.shape[1]
    sub = lax.broadcasted_iota(jnp.int32, (n_blocks, 128), 0)
    lane = lax.broadcasted_iota(jnp.int32, (n_blocks, 128), 1)
    sub_sq = lax.broadcasted_iota(jnp.int32, (n_blocks, n_blocks), 0)
    lane_sq = lax.broadcasted_iota(jnp.int32, (n_blocks, n_blocks), 1)
    diag = jnp.where(sub_sq == lane_sq, jnp.broadcast_to(tgt_v[...], sub_sq.shape), 0)
    named = jnp.sum(diag, axis=1, keepdims=True) == lane
    band = sub // COLBLK
    side = lax.rem(band, 2)
    local = jnp.where(side == side_here, sub - (band - band // 2) * COLBLK, 0)
    for i, code in enumerate((local, side, jnp.ones_like(sub))):
        tbl_v[i : i + 1, :] = jnp.max(jnp.where(named, code, 0), axis=0, keepdims=True)
    tbl_copy = pltpu.make_async_copy(tbl_v, tbl, in_sem.at[9])
    tbl_copy.start()

    with jax.named_scope("barrier"):
        pl.semaphore_wait(barrier, len(peers))

    def send(src, dst, ssem, rsem, pf, pq=q):
        pltpu.make_async_remote_copy(
            src_ref=src,
            dst_ref=dst,
            send_sem=ssem,
            recv_sem=rsem,
            device_id=(pf, pq),
            device_id_type=MESH,
        ).start()

    def wait_bytes(ref, sem):
        pltpu.make_async_copy(ref, ref, sem).wait()

    def some(ref, n):
        return ref.at[pl.ds(0, n)]

    def all_but_one(ref):
        return some(ref, ref.shape[0] - 1)

    def g_spread(r):
        rows = g_v[r * RC : (r + 1) * RC, :]
        for xx in range(NX):
            for j in range(COLBLK):
                lo = j * BLOCK + xx * LANE
                xs[r, xx, j] = rows[:, lo : lo + LANE]
        for d in X_ORDER:
            px = rot(x, d, NX)
            send(xs.at[r, px], xr[r].at[x], xsend.at[0, r], xrecv.at[0, r], fid(px, z, c))
        xr[r][x] = xs[r, x]

    def g_exchange(r):
        with jax.named_scope("g_spread_wait"):
            wait_bytes(all_but_one(xr[r]), xrecv.at[0, r])

        def slots(pz, dst):
            for s in range(SLOTS):
                l = tbl[0, fid(s // NC, pz, s % NC)]
                dst[s] = xr[r][l // COLBLK, lax.rem(l, COLBLK)]

        for d in Z_ORDER:
            pz = rot(z, d, NZ)
            slots(pz, zs.at[r, pz])
            send(zs.at[r, pz], zr[r].at[z], zsend.at[0, r], zrecv.at[0, r], fid(x, pz, c))
        slots(z, zr[r].at[z])

    def g_gather(r):
        with jax.named_scope("g_exchange_wait"):
            wait_bytes(all_but_one(zr[r]), zrecv.at[0, r])
        for s in range(SLOTS):
            h = tbl[1, fid(s // NC, z, s % NC)]
            for i in range(HALF):
                gs[r, s, i] = zr[r][h * HALF + i, s]
        for dx, dc in near:
            px, pc = rot(x, dx, NX), rot(c, dc, NC)
            send(
                gs.at[r, px * NC + pc],
                gr.at[r, x, c],
                gsend.at[0, r],
                grecv.at[0, r],
                fid(px, z, pc),
            )
        gr[r, x, c] = gs[r, x * NC + c]

    def g_assemble(r):
        with jax.named_scope("g_gather_wait"):
            wait_bytes(all_but_one(gs.at[r]), grecv.at[0, r])
        for xx in range(NX):
            for cc in range(NC):
                for i in range(HALF):
                    blk[0, i * NC + cc, r * RC : (r + 1) * RC, xx * LANE : (xx + 1) * LANE] = gr[
                        r, xx, cc, i
                    ]

    def m_spread(r):
        for d in X_ORDER:
            send(ms.at[r], mx[r].at[x], xsend.at[1, r], xrecv.at[1, r], fid(rot(x, d, NX), z, c))
        mx[r][x] = ms[r]

    def m_exchange(r):
        with jax.named_scope("m_spread_wait"):
            wait_bytes(all_but_one(mx[r]), xrecv.at[1, r])

        def slot(pz, pc, dst):
            l = tbl[0, fid(x, pz, pc)]
            dst[...] = mx[r][l // COLBLK, lax.rem(l, COLBLK)]

        for d in Z_ORDER + (0,):
            pz = rot(z, d, NZ)
            for dc in range(NC):
                pc = rot(c, dc, NC)
                if d or dc:
                    slot(pz, pc, mzs.at[r, pz * NC + pc])
                    send(
                        mzs.at[r, pz * NC + pc],
                        mz[r].at[z * NC + c],
                        zsend.at[1, r],
                        zrecv.at[1, r],
                        fid(x, pz, pc),
                    )
        slot(z, c, mz[r].at[z * NC + c])


    def m_assemble(r):
        with jax.named_scope("m_exchange_wait"):
            wait_bytes(all_but_one(mz[r]), zrecv.at[1, r])
        h = tbl[1, f]
        for i in range(HALF):
            for cc in range(NC):
                blk[1, i * NC + cc, r * RC : (r + 1) * RC, :] = mz[r][(h * HALF + i) * NC + cc]

    def d_exchange(r, upd):
        for i in range(HALF):
            for cc in range(NC):
                lo = (i * NC + cc) * RC
                uds[r, i, cc] = upd[lo : lo + RC, :]
        for d in Z_ORDER + (0,):
            pz = rot(z, d, NZ)
            for dc in range(NC):
                pc = rot(c, dc, NC)
                if d or dc:
                    send(
                        uds.at[r, lax.rem(pz, HALF), pc],
                        udz[r].at[z * NC + c],
                        zsend.at[2, r],
                        zrecv.at[2, r],
                        fid(x, pz, pc),
                    )
        udz[r][z * NC + c] = uds[r, lax.rem(z, HALF), c]

    def d_gather(r):
        with jax.named_scope("d_exchange_wait"):
            wait_bytes(all_but_one(udz[r]), zrecv.at[2, r])
        for d in X_ORDER + (0,):
            px = rot(x, d, NX)
            for j in range(COLBLK):
                t = tgt_s[0, (px * 2 + side_here) * COLBLK + j]
                part = udz[r][lax.rem(t, NZ * NC)]
                if d:
                    udp[r, px, j] = part
                else:
                    udx[r][x, j] = part
            if d:
                send(udp.at[r, px], udx[r].at[x], xsend.at[2, r], xrecv.at[2, r], fid(px, z, c))

    def d_finish(r):
        with jax.named_scope("d_gather_wait"):
            wait_bytes(all_but_one(udx[r]), xrecv.at[2, r])
        for j in range(COLBLK):
            t = tgt_s[0, (x * 2 + side_here) * COLBLK + j]
            out_v[r * RC : (r + 1) * RC, j * BLOCK : (j + 1) * BLOCK] = udx[r][t // (NZ * NC), j]

    me = x * NC + c

    def u_spread(r, upd):
        for xx in range(NX):
            for cc in range(NC):
                for i in range(HALF):
                    lo = (i * NC + cc) * RC
                    ub[r, xx, cc, i] = upd[lo : lo + RC, xx * LANE : (xx + 1) * LANE]
        for dx, dc in near:
            px, pc = rot(x, dx, NX), rot(c, dc, NC)
            send(ub.at[r, px, pc], ug.at[r, me], gsend.at[2, r], grecv.at[2, r], fid(px, z, pc))
        ug[r, me] = ub[r, x, c]

    def u_exchange(r):
        with jax.named_scope("u_spread_wait"):
            wait_bytes(all_but_one(ug.at[r]), grecv.at[2, r])
        for d in Z_ORDER:
            pz = rot(z, d, NZ)
            send(
                ug.at[r, :, lax.rem(pz, HALF)],
                uz[r].at[z],
                zsend.at[2, r],
                zrecv.at[2, r],
                fid(x, pz, c),
            )
        for s in range(SLOTS):
            uz[r][z, s] = ug[r, s, lax.rem(z, HALF)]

    def u_gather(r):
        with jax.named_scope("u_exchange_wait"):
            wait_bytes(all_but_one(uz[r]), zrecv.at[2, r])
        for d in X_ORDER + (0,):
            px = rot(x, d, NX)
            for j in range(COLBLK):
                t = tgt_s[0, (px * 2 + side_here) * COLBLK + j]
                slot = (t // (NC * NZ)) * NC + lax.rem(t, NC)
                part = uz[r][lax.rem(t // NC, NZ), slot]
                if d:
                    us[r, px, j] = part
                else:
                    uf[r, x, j] = part
            if d:
                send(us.at[r, px], uf.at[r, x], xsend.at[2, r], xrecv.at[2, r], fid(px, z, c))

    def u_finish(r):
        with jax.named_scope("u_gather_wait"):
            wait_bytes(all_but_one(uf.at[r]), xrecv.at[2, r])
        for xx in range(NX):
            for j in range(COLBLK):
                lo = j * BLOCK + xx * LANE
                out_v[r * RC : (r + 1) * RC, lo : lo + LANE] = uf[r, xx, j]

    loads[0].wait()
    g_spread(0)
    wide = g_v[...].astype(F32)
    cols = jnp.sum((wide * wide).reshape(ROWS // 8, 8, wide.shape[1]), axis=0)
    acc = cols[:, :128]
    for i in range(1, cols.shape[1] // 128):
        acc = acc + cols[:, i * 128 : (i + 1) * 128]
    norm_s[0] = acc
    norm_y[q] = acc
    for d in range(1, n_mp):
        send(norm_s.at[0], norm_y.at[q], nsend.at[0], nrecv.at[0], f, rot(q, d, n_mp))
    g_spread(1)
    tbl_copy.wait()
    g_exchange(0)
    g_spread(2)

    wait_bytes(all_but_one(norm_y), nrecv.at[0])
    acc = jnp.sum(norm_y[...], axis=0)
    norm_s[1] = acc
    norm_x[me] = acc
    for dx, dc in near:
        send(
            norm_s.at[1],
            norm_x.at[me],
            nsend.at[1],
            nrecv.at[1],
            fid(rot(x, dx, NX), z, rot(c, dc, NC)),
        )
    g_exchange(1)
    g_spread(3)
    with jax.named_scope("norm_x_wait"):
        wait_bytes(all_but_one(norm_x), nrecv.at[1])
    acc = jnp.sum(norm_x[...], axis=0)
    norm_s[2] = acc
    norm_z[z] = acc
    for d in Z_ORDER:
        send(norm_s.at[2], norm_z.at[z], nsend.at[2], nrecv.at[2], fid(x, rot(z, d, NZ), c))
    g_exchange(2)
    g_exchange(3)
    with jax.named_scope("norm_z_wait"):
        wait_bytes(all_but_one(norm_z), nrecv.at[2])
    acc = jnp.sum(norm_z[...], axis=0)
    norm_sum = jnp.sum(jnp.sum(acc, axis=0, keepdims=True), axis=1, keepdims=True)
    clip = jnp.minimum(1.0, CLIP_RMS * (float(n_entries) ** 0.5) / jnp.sqrt(norm_sum))

    loads[1].wait()
    for r in range(CHUNKS):
        rows = slice(r * RC, (r + 1) * RC)
        nxt = FIRST_DECAY * f_v[rows, :] + ((1.0 - FIRST_DECAY) * clip) * g_v[rows, :].astype(F32)
        f_v[rows, :] = nxt
        low = nxt.astype(BF16)
        for j in range(COLBLK):
            ms[r, j] = low[:, j * BLOCK : (j + 1) * BLOCK]
        if r < 2:
            m_spread(r)
    for load in loads[2:]:
        load.wait()
    qlt_v[...] = ql_v[...].reshape(BLOCK, BLOCK).T
    qrt_v[...] = qr_v[...].T
    g_gather(0)
    m_exchange(0)
    m_spread(2)
    g_gather(1)
    m_exchange(1)
    m_spread(3)
    g_gather(2)
    m_exchange(2)
    g_gather(3)
    m_exchange(3)

    for r in range(CHUNKS):
        g_assemble(r)
    with jax.named_scope("owner_gradient"):
        live = tbl[2, f] > 0
        block = blk[0].reshape(BLOCK, BLOCK)
        half = mm(qlt_v[...], block).astype(BF16)
        rotated = clip * mm(half, qr_v[...])
        second = SECOND_DECAY * sm_v[...] + SECOND_RATE * rotated * rotated
        den_v[...] = jnp.sqrt(second) + EPSILON
        sm_v[...] = jnp.where(live, second, sm_v[...])
        scale = GRAM_RATE * clip * clip / BLOCK
        block_t = block.T
        lg_v[...] = jnp.where(live, GRAM_DECAY * lg_v[...] + scale * mm(block, block_t), lg_v[...])
        rg_v[...] = jnp.where(live, GRAM_DECAY * rg_v[...] + scale * mm(block_t, block), rg_v[...])

    for r in range(CHUNKS):
        m_assemble(r)
    with jax.named_scope("owner_moment"):
        mhalf = mm(qlt_v[...], blk[1].reshape(BLOCK, BLOCK)).astype(BF16)
        normed = (mm(mhalf, qr_v[...]) / den_v[...]).astype(BF16)
    for r in range(CHUNKS):
        rows = ql_v[:, r * RC : (r + 1) * RC, :].reshape(HALF * NC * RC, BLOCK)
        upd = mm(mm(rows, normed).astype(BF16), qrt_v[...]).astype(BF16)
        if r < DIRECT:
            d_exchange(r, upd)
        else:
            u_spread(r, upd)
    for r in range(DIRECT, CHUNKS):
        u_exchange(r)
    for r in range(DIRECT):
        d_gather(r)
    for r in range(DIRECT, CHUNKS):
        u_gather(r)
    for r in range(DIRECT):
        d_finish(r)
    for r in range(DIRECT, CHUNKS):
        u_finish(r)

    wait_bytes(all_but_one(norm_y), nsend.at[0])
    wait_bytes(all_but_one(norm_x), nsend.at[1])
    wait_bytes(all_but_one(norm_z), nsend.at[2])
    for r in range(CHUNKS):
        wait_bytes(all_but_one(xr[r]), xsend.at[0, r])
        wait_bytes(all_but_one(zr[r]), zsend.at[0, r])
        wait_bytes(all_but_one(gs.at[r]), gsend.at[0, r])
        wait_bytes(all_but_one(mx[r]), xsend.at[1, r])
        wait_bytes(all_but_one(mz[r]), zsend.at[1, r])
        if r < DIRECT:
            wait_bytes(all_but_one(udz[r]), zsend.at[2, r])
            wait_bytes(all_but_one(udx[r]), xsend.at[2, r])
        else:
            wait_bytes(all_but_one(ug.at[r]), gsend.at[2, r])
            wait_bytes(all_but_one(uz[r]), zsend.at[2, r])
            wait_bytes(all_but_one(uf.at[r]), xsend.at[2, r])


def write_out(*refs):
    n = (len(refs) - 1) // 2
    copies = [
        pltpu.make_async_copy(refs[i], refs[n + i], refs[-1].at[i]) for i in range(n)
    ]
    for copy in copies:
        copy.start()
    for copy in copies:
        copy.wait()


def shards(
    gradient,
    first_moment,
    left_gram,
    right_gram,
    left_basis,
    right_basis,
    second_moment,
    block_target,
):
    rows, cols = gradient.shape
    n_fsdp = lax.axis_size("fsdp")
    n_mp = lax.axis_size("mp")
    n_blocks = block_target.shape[1]
    any_spec = pl.BlockSpec(memory_space=pl.ANY)
    vmem_spec = pl.BlockSpec(memory_space=pltpu.VMEM)
    vm = pltpu.VMEM
    dma = pltpu.SemaphoreType.DMA
    mat = (BLOCK, BLOCK)
    piece = (RC, LANE)
    strip = (RC, BLOCK)

    def per_chunk(n, *shape):
        return [vm(shape, BF16) for _ in range(n)]

    shapes = [((rows, cols), BF16), ((rows, cols), F32)] + [(mat, F32)] * 3
    held = pl.pallas_call(
        functools.partial(kernel, rows * cols * n_fsdp * n_mp),
        out_shape=tuple(vm(s, d) for s, d in shapes),
        in_specs=[any_spec] * 8,
        out_specs=(vmem_spec,) * 5,
        scratch_shapes=[
            vm((rows, cols), BF16),
            vm((HALF * NC, ROWS, BLOCK), BF16),
            vm(mat, BF16),
            vm(mat, BF16),
            vm(mat, BF16),
            vm(mat, F32),
            vm((3, 8, 128), F32),
            vm((n_mp, 8, 128), F32),
            vm((SLOTS, 8, 128), F32),
            vm((NZ, 8, 128), F32),
            vm((CHUNKS, NX, COLBLK) + piece, BF16),
            per_chunk(CHUNKS, NX, COLBLK, *piece),
            vm((CHUNKS, NZ, SLOTS) + piece, BF16),
            per_chunk(CHUNKS, NZ, SLOTS, *piece),
            vm((CHUNKS, SLOTS, HALF) + piece, BF16),
            vm((CHUNKS, NX, NC, HALF) + piece, BF16),
            vm((2, HALF * NC, ROWS, BLOCK), BF16),
            vm((CHUNKS, COLBLK) + strip, BF16),
            per_chunk(CHUNKS, NX, COLBLK, *strip),
            vm((CHUNKS, NZ * NC) + strip, BF16),
            per_chunk(CHUNKS, NZ * NC, *strip),
            vm((DIRECT, HALF, NC) + strip, BF16),
            per_chunk(DIRECT, NZ * NC, *strip),
            vm((DIRECT, NX, COLBLK) + strip, BF16),
            per_chunk(DIRECT, NX, COLBLK, *strip),
            vm((CHUNKS, NX, NC, HALF) + piece, BF16),
            vm((CHUNKS, SLOTS, HALF) + piece, BF16),
            per_chunk(CHUNKS, NZ, SLOTS, *piece),
            vm((CHUNKS, NX, COLBLK) + piece, BF16),
            vm((CHUNKS, NX, COLBLK) + piece, BF16),
            pltpu.SMEM((1, n_blocks), jnp.int32),
            vm((1, n_blocks), jnp.int32),
            vm((8, 128), jnp.int32),
            pltpu.SMEM((8, 128), jnp.int32),
            dma((10,)),
            dma((3,)),
            dma((3,)),
        ]
        + [dma((3, CHUNKS))] * 6,
        compiler_params=pltpu.CompilerParams(
            collective_id=0, has_side_effects=True, vmem_limit_bytes=59 * 2**20
        ),
        cost_estimate=pl.CostEstimate(
            flops=16 * BLOCK**3, bytes_accessed=12 * 2**20, transcendentals=BLOCK**2
        ),
    )(
        block_target,
        gradient,
        first_moment,
        left_gram[0, 0],
        right_gram[0, 0],
        left_basis[0, 0].reshape(HALF * NC, ROWS, BLOCK),
        right_basis[0, 0],
        second_moment[0, 0],
    )
    out = pl.pallas_call(
        write_out,
        out_shape=tuple(jax.ShapeDtypeStruct(s, d) for s, d in shapes),
        in_specs=[vmem_spec] * 5,
        out_specs=(any_spec,) * 5,
        scratch_shapes=[dma((5,))],
        compiler_params=pltpu.CompilerParams(vmem_limit_bytes=2**20),
    )(*held)
    return (out[0], out[1]) + tuple(o[None, None] for o in out[2:])


def solution(mesh):
    return jax.shard_map(
        shards,
        mesh=mesh,
        in_specs=(
            P("fsdp", "mp"),
            P("fsdp", "mp"),
            P("fsdp", "mp", None, None),
            P("fsdp", "mp", None, None),
            P("fsdp", "mp", None, None),
            P("fsdp", "mp", None, None),
            P("fsdp", "mp", None, None),
            P("mp", None),
        ),
        out_specs=(
            P("fsdp", "mp"),
            P("fsdp", "mp"),
            P("fsdp", "mp", None, None),
            P("fsdp", "mp", None, None),
            P("fsdp", "mp", None, None),
        ),
        check_vma=False,
    )
```

```python
import functools
import math

import jax
import jax.numpy as jnp
from jax import lax
from jax.experimental import pallas as pl
from jax.experimental.pallas import tpu as pltpu
from jax.sharding import PartitionSpec as P

CLIP_RMS = 0.5
FIRST_DECAY = 0.9
GRAM_DECAY = 0.95
GRAM_RATE = 0.05
SECOND_DECAY = 0.95
SECOND_RATE = 0.05
EPSILON = 1e-08

MESH = pl.DeviceIdType.MESH
NX, NZ, NC = 4, 8, 2
HALF = NZ // 2
COLBLK = 7
SLOTS = NX * NC
LOCAL = NX * COLBLK
ROWS = 64
BLOCK = 512
LANE = BLOCK // NX
CHUNKS = 4
FOLD = 2
DIRECT = 1
RC = ROWS // CHUNKS
Z_ORDER = (4, 5, 3, 6, 2, 7, 1)
X_ORDER = (2, 1, 3)

UNIT = RC * LANE * 2
PLAIN = [(a, r) for a in range(2) for r in range(FOLD)]
LATER = [(1, r) for r in range(FOLD, CHUNKS)] + [(2, 0), (2, 1)]
RECV = [(k,) + ar for k in "xz" for ar in PLAIN + LATER]
RECV += [("g",) + ar for ar in PLAIN + [(2, 1)]]
RECV += [("f", i) for i in range(8)] + [("n", i) for i in range(3)]

BF16, F32 = jnp.bfloat16, jnp.float32


def mm(a, b):
    return jnp.dot(a, b, preferred_element_type=F32)


def kernel(
    n_entries,
    tgt_hbm,
    grad_hbm,
    first_hbm,
    lg_hbm,
    rg_hbm,
    ql_hbm,
    qr_hbm,
    sm_hbm,
    out_v,
    f_v,
    lg_v,
    rg_v,
    sm_v,
    g_v,
    ql_v,
    qr_v,
    qlt_v,
    qrt_v,
    den_v,
    norm_s,
    norm_y,
    norm_x,
    norm_z,
    xs,
    xr,
    zs,
    zr,
    gs,
    gr,
    fx,
    fs,
    fr,
    fzs,
    fz,
    fg,
    blk,
    ms,
    mx,
    mzs,
    mz,
    uds,
    udz,
    udp,
    udx,
    fub,
    fug,
    fuz,
    fus,
    fuf,
    fsw,
    fsr,
    ub,
    ug,
    uz,
    us,
    uf,
    tgt_s,
    tgt_v,
    tbl_v,
    tbl,
    units,
    in_sem,
    send_sem,
    recv_sem,
):
    f = lax.axis_index("fsdp")
    q = lax.axis_index("mp")
    c = lax.rem(f, NC)
    z = lax.rem(f // NC, NZ)
    x = f // (NC * NZ)
    side_here = z // HALF
    n_mp = lax.axis_size("mp")

    def fid(xx, zz, cc):
        return (xx * NZ + zz) * NC + cc

    def rot(v, d, n):
        return lax.rem(v + d, n)

    near = [(dx, dc) for dx in X_ORDER + (0,) for dc in range(NC) if dx or dc]
    barrier = pltpu.get_barrier_semaphore()
    peers = [(fid(x, rot(z, d, NZ), rot(c, dc, NC)), q) for d in Z_ORDER for dc in range(NC)]
    peers += [(fid(rot(x, dx, NX), z, rot(c, dc, NC)), q) for dx, dc in near]
    peers += [(f, rot(q, d, n_mp)) for d in range(1, n_mp)]
    for peer in peers:
        pl.semaphore_signal(barrier, inc=1, device_id=peer, device_id_type=MESH)

    tgt_loads = [
        pltpu.make_async_copy(tgt_hbm, tgt_s, in_sem.at[3]),
        pltpu.make_async_copy(tgt_hbm, tgt_v, in_sem.at[4]),
    ]
    loads = [
        pltpu.make_async_copy(src, dst, in_sem.at[min(i, 2)])
        for i, (src, dst) in enumerate(
            (
                (grad_hbm, g_v),
                (first_hbm, f_v),
                (ql_hbm, ql_v),
                (qr_hbm, qr_v),
                (sm_hbm, sm_v),
                (lg_hbm, lg_v),
                (rg_hbm, rg_v),
            )
        )
    ]
    for load in loads[:1] + tgt_loads + loads[1:]:
        load.start()

    loads[0].wait()
    wide = g_v[...].astype(F32)
    cols = jnp.sum((wide * wide).reshape(ROWS // 8, 8, wide.shape[1]), axis=0)
    acc = cols[:, :128]
    for i in range(1, cols.shape[1] // 128):
        acc = acc + cols[:, i * 128 : (i + 1) * 128]
    norm_s[0] = acc
    norm_z[z] = acc

    with jax.named_scope("barrier"):
        pl.semaphore_wait(barrier, len(peers))

    sent = [0, 0, 0]
    group = [0]

    def send(src, dst, rsem, pf, pq=q, under=None):
        under = group[0] if under is None else under
        sent[under] += math.prod(src.shape) * src.dtype.itemsize // UNIT
        pltpu.make_async_remote_copy(
            src_ref=src,
            dst_ref=dst,
            send_sem=send_sem.at[under],
            recv_sem=rsem,
            device_id=(pf, pq),
            device_id_type=MESH,
        ).start()

    def recv(*key):
        return recv_sem.at[RECV.index(key)]

    def wait_units(n, sem):
        wait_bytes(units.at[pl.ds(0, n)], sem)

    def wait_bytes(ref, sem):
        pltpu.make_async_copy(ref, ref, sem).wait()

    def some(ref, n):
        return ref.at[pl.ds(0, n)]

    def all_but_one(ref):
        return some(ref, ref.shape[0] - 1)

    def p_spread(a, r, rows):
        for xx in range(NX):
            for j in range(COLBLK):
                lo = j * BLOCK + xx * LANE
                xs[a, r, xx, j] = rows[:, lo : lo + LANE]
        for d in X_ORDER:
            px = rot(x, d, NX)
            send(xs.at[a, r, px], xr[a][r].at[x], recv("x", a, r), fid(px, z, c))
        xr[a][r][x] = xs[a, r, x]

    def p_exchange(a, r):
        with jax.named_scope("p_spread_wait"):
            wait_bytes(all_but_one(xr[a][r]), recv("x", a, r))

        def slots(pz, dst):
            for s in range(SLOTS):
                l = tbl[0, fid(s // NC, pz, s % NC)]
                dst[s] = xr[a][r][l // COLBLK, lax.rem(l, COLBLK)]

        for d in Z_ORDER:
            pz = rot(z, d, NZ)
            slots(pz, zs.at[a, r, pz])
            send(zs.at[a, r, pz], zr[a][r].at[z], recv("z", a, r), fid(x, pz, c))
        slots(z, zr[a][r].at[z])

    def p_gather(a, r):
        with jax.named_scope("p_exchange_wait"):
            wait_bytes(all_but_one(zr[a][r]), recv("z", a, r))
        for s in range(SLOTS):
            h = tbl[1, fid(s // NC, z, s % NC)]
            for i in range(HALF):
                gs[a, r, s, i] = zr[a][r][h * HALF + i, s]
        for dx, dc in near:
            px, pc = rot(x, dx, NX), rot(c, dc, NC)
            send(
                gs.at[a, r, px * NC + pc],
                gr.at[a, r, x, c],
                recv("g", a, r),
                fid(px, z, pc),
            )
        gr[a, r, x, c] = gs[a, r, x * NC + c]

    def p_assemble(a, r):
        with jax.named_scope("p_gather_wait"):
            wait_bytes(all_but_one(gs.at[a, r]), recv("g", a, r))
        for xx in range(NX):
            for cc in range(NC):
                for i in range(HALF):
                    blk[a, i * NC + cc, r * RC : (r + 1) * RC, xx * LANE : (xx + 1) * LANE] = gr[
                        a, r, xx, cc, i
                    ]

    mate = fid(x, rot(z, HALF, NZ), c)

    def f_swap():
        src = g_v.at[pl.ds(pl.multiple_of((FOLD + 1 - side_here) * RC, RC), RC), :]
        send(src, fx, recv("f", 0), mate)

    def f_spread():
        with jax.named_scope("f_swap_wait"):
            wait_bytes(fx, recv("f", 0))
        mine = g_v[pl.ds(pl.multiple_of((FOLD + side_here) * RC, RC), RC), :]
        theirs = fx[...]
        for xx in range(NX):
            for j in range(COLBLK):
                lo = j * BLOCK + xx * LANE
                fs[xx, side_here, j] = mine[:, lo : lo + LANE]
                fs[xx, 1 - side_here, j] = theirs[:, lo : lo + LANE]
        for d in X_ORDER:
            px = rot(x, d, NX)
            for h in range(2):
                send(
                    fs.at[px, h],
                    fr.at[pl.ds((x * 2 + h) * COLBLK, COLBLK)],
                    recv("f", 1),
                    fid(px, z, c),
                )
        for h in range(2):
            fr[pl.ds((x * 2 + h) * COLBLK, COLBLK)] = fs[x, h]

    def f_exchange():
        with jax.named_scope("f_spread_wait"):
            wait_bytes(some(fr, 2 * COLBLK * (NX - 1)), recv("f", 1))

        def slots(pz, dst):
            for s in range(SLOTS):
                dst[s] = fr[tbl[3, fid(s // NC, pz, s % NC)]]

        for d in Z_ORDER:
            pz = rot(z, d, NZ)
            slots(pz, fzs.at[pz])
            send(fzs.at[pz], fz.at[z], recv("f", 2), fid(x, pz, c))
        slots(z, fz.at[z])

    def f_gather():
        with jax.named_scope("f_exchange_wait"):
            wait_bytes(all_but_one(fz), recv("f", 2))
        for dx, dc in near:
            px, pc = rot(x, dx, NX), rot(c, dc, NC)
            send(fz.at[:, px * NC + pc], fg.at[x, c], recv("f", 3), fid(px, z, pc))
        for i in range(NZ):
            fg[x, c, i] = fz[i, x * NC + c]

    def f_assemble():
        with jax.named_scope("f_gather_wait"):
            wait_bytes(some(fz, NZ - 1), recv("f", 3))
        for xx in range(NX):
            for cc in range(NC):
                for i in range(NZ):
                    lo = (FOLD + i // HALF) * RC
                    blk[0, i % HALF * NC + cc, lo : lo + RC, xx * LANE : (xx + 1) * LANE] = fg[
                        xx, cc, i
                    ]

    def m_spread(r):
        for d in X_ORDER:
            send(ms.at[r], mx[r].at[x], recv("x", 1, FOLD + r), fid(rot(x, d, NX), z, c))
        mx[r][x] = ms[r]

    def m_exchange(r):
        with jax.named_scope("m_spread_wait"):
            wait_bytes(all_but_one(mx[r]), recv("x", 1, FOLD + r))

        def slot(pz, pc, dst):
            l = tbl[0, fid(x, pz, pc)]
            dst[...] = mx[r][l // COLBLK, lax.rem(l, COLBLK)]

        for d in Z_ORDER + (0,):
            pz = rot(z, d, NZ)
            for dc in range(NC):
                pc = rot(c, dc, NC)
                if d or dc:
                    slot(pz, pc, mzs.at[r, pz * NC + pc])
                    send(
                        mzs.at[r, pz * NC + pc],
                        mz[r].at[z * NC + c],
                        recv("z", 1, FOLD + r),
                        fid(x, pz, pc),
                    )
        slot(z, c, mz[r].at[z * NC + c])


    def m_assemble(r):
        with jax.named_scope("m_exchange_wait"):
            wait_bytes(all_but_one(mz[r]), recv("z", 1, FOLD + r))
        h = tbl[1, f]
        for i in range(HALF):
            for cc in range(NC):
                lo = (FOLD + r) * RC
                blk[1, i * NC + cc, lo : lo + RC, :] = mz[r][(h * HALF + i) * NC + cc]

    def d_exchange(r, upd):
        for i in range(HALF):
            for cc in range(NC):
                lo = (i * NC + cc) * RC
                uds[r, i, cc] = upd[lo : lo + RC, :]
        for d in Z_ORDER + (0,):
            pz = rot(z, d, NZ)
            for dc in range(NC):
                pc = rot(c, dc, NC)
                if d or dc:
                    send(
                        uds.at[r, lax.rem(pz, HALF), pc],
                        udz[r].at[z * NC + c],
                        recv("z", 2, r),
                        fid(x, pz, pc),
                    )
        udz[r][z * NC + c] = uds[r, lax.rem(z, HALF), c]

    def d_gather(r):
        with jax.named_scope("d_exchange_wait"):
            wait_bytes(all_but_one(udz[r]), recv("z", 2, r))
        for d in X_ORDER + (0,):
            px = rot(x, d, NX)
            for j in range(COLBLK):
                t = tgt_s[0, (px * 2 + side_here) * COLBLK + j]
                part = udz[r][lax.rem(t, NZ * NC)]
                if d:
                    udp[r, px, j] = part
                else:
                    udx[r][x, j] = part
            if d:
                send(udp.at[r, px], udx[r].at[x], recv("x", 2, r), fid(px, z, c))

    def d_finish(r):
        with jax.named_scope("d_gather_wait"):
            wait_bytes(all_but_one(udx[r]), recv("x", 2, r))
        for j in range(COLBLK):
            t = tgt_s[0, (x * 2 + side_here) * COLBLK + j]
            out_v[r * RC : (r + 1) * RC, j * BLOCK : (j + 1) * BLOCK] = udx[r][t // (NZ * NC), j]

    me = x * NC + c

    def u_spread(r, upd):
        for xx in range(NX):
            for cc in range(NC):
                for i in range(HALF):
                    lo = (i * NC + cc) * RC
                    ub[r, xx, cc, i] = upd[lo : lo + RC, xx * LANE : (xx + 1) * LANE]
        for dx, dc in near:
            px, pc = rot(x, dx, NX), rot(c, dc, NC)
            send(ub.at[r, px, pc], ug.at[r, me], recv("g", 2, r), fid(px, z, pc))
        ug[r, me] = ub[r, x, c]

    def u_exchange(r):
        with jax.named_scope("u_spread_wait"):
            wait_bytes(all_but_one(ug.at[r]), recv("g", 2, r))
        for d in Z_ORDER:
            pz = rot(z, d, NZ)
            send(
                ug.at[r, :, lax.rem(pz, HALF)],
                uz[r].at[z],
                recv("z", 2, r),
                fid(x, pz, c),
            )
        for s in range(SLOTS):
            uz[r][z, s] = ug[r, s, lax.rem(z, HALF)]

    def u_gather(r):
        with jax.named_scope("u_exchange_wait"):
            wait_bytes(all_but_one(uz[r]), recv("z", 2, r))
        for d in X_ORDER + (0,):
            px = rot(x, d, NX)
            for j in range(COLBLK):
                t = tgt_s[0, (px * 2 + side_here) * COLBLK + j]
                slot = (t // (NC * NZ)) * NC + lax.rem(t, NC)
                part = uz[r][lax.rem(t // NC, NZ), slot]
                if d:
                    us[r, px, j] = part
                else:
                    uf[r, x, j] = part
            if d:
                send(us.at[r, px], uf.at[r, x], recv("x", 2, r), fid(px, z, c))

    def u_finish(r):
        with jax.named_scope("u_gather_wait"):
            wait_bytes(all_but_one(uf.at[r]), recv("x", 2, r))
        for xx in range(NX):
            for j in range(COLBLK):
                lo = j * BLOCK + xx * LANE
                out_v[r * RC : (r + 1) * RC, lo : lo + LANE] = uf[r, xx, j]

    def uf_spread(upds):
        for h in range(2):
            for xx in range(NX):
                for cc in range(NC):
                    for i in range(HALF):
                        lo = (i * NC + cc) * RC
                        fub[xx, cc, h * HALF + i] = upds[h][
                            lo : lo + RC, xx * LANE : (xx + 1) * LANE
                        ]
        for dx, dc in near:
            px, pc = rot(x, dx, NX), rot(c, dc, NC)
            send(fub.at[px, pc], fug.at[me], recv("f", 4), fid(px, z, pc))
        fug[me] = fub[x, c]

    def uf_exchange():
        with jax.named_scope("uf_spread_wait"):
            wait_bytes(all_but_one(fug), recv("f", 4))
        for d in Z_ORDER:
            pz = rot(z, d, NZ)
            send(fug.at[:, pz], fuz.at[z], recv("f", 5), fid(x, pz, c), under=2)
        for s in range(SLOTS):
            fuz[z, s] = fug[s, z]

    def uf_gather():
        with jax.named_scope("uf_exchange_wait"):
            wait_bytes(all_but_one(fuz), recv("f", 5))
        for d in X_ORDER + (0,):
            px = rot(x, d, NX)
            for h in range(2):
                for j in range(COLBLK):
                    t = tgt_s[0, (px * 2 + h) * COLBLK + j]
                    slot = (t // (NC * NZ)) * NC + lax.rem(t, NC)
                    part = fuz[lax.rem(t // NC, NZ), slot]
                    if d:
                        fus[px, h, j] = part
                    else:
                        fuf[x, h, j] = part
            if d:
                send(fus.at[px], fuf.at[x], recv("f", 6), fid(px, z, c))

    def uf_swap():
        with jax.named_scope("uf_gather_wait"):
            wait_bytes(all_but_one(fuf), recv("f", 6))
        for xx in range(NX):
            for j in range(COLBLK):
                lo = j * BLOCK + xx * LANE
                fsw[:, lo : lo + LANE] = fuf[xx, 1 - side_here, j]
        send(fsw, fsr, recv("f", 7), mate)
        rows = pl.ds(pl.multiple_of((FOLD + side_here) * RC, RC), RC)
        for xx in range(NX):
            for j in range(COLBLK):
                lo = j * BLOCK + xx * LANE
                out_v[rows, lo : lo + LANE] = fuf[xx, side_here, j]

    def uf_finish():
        with jax.named_scope("uf_swap_wait"):
            wait_bytes(fsr, recv("f", 7))
        out_v[pl.ds(pl.multiple_of((FOLD + 1 - side_here) * RC, RC), RC), :] = fsr[...]

    for d in Z_ORDER:
        send(norm_s.at[0], norm_z.at[z], recv("n", 0), fid(x, rot(z, d, NZ), c))
    p_spread(0, 0, g_v[:RC, :])
    f_swap()
    p_spread(0, 1, g_v[RC : 2 * RC, :])

    for load in tgt_loads:
        load.wait()
    n_blocks = tgt_v.shape[1]
    sub = lax.broadcasted_iota(jnp.int32, (n_blocks, 128), 0)
    lane = lax.broadcasted_iota(jnp.int32, (n_blocks, 128), 1)
    sub_sq = lax.broadcasted_iota(jnp.int32, (n_blocks, n_blocks), 0)
    lane_sq = lax.broadcasted_iota(jnp.int32, (n_blocks, n_blocks), 1)
    diag = jnp.where(sub_sq == lane_sq, jnp.broadcast_to(tgt_v[...], sub_sq.shape), 0)
    named = jnp.sum(diag, axis=1, keepdims=True) == lane
    band = sub // COLBLK
    side = lax.rem(band, 2)
    local = jnp.where(side == side_here, sub - (band - band // 2) * COLBLK, 0)
    for i, code in enumerate((local, side, jnp.ones_like(sub), sub)):
        tbl_v[i : i + 1, :] = jnp.max(jnp.where(named, code, 0), axis=0, keepdims=True)
    tbl_copy = pltpu.make_async_copy(tbl_v, tbl, in_sem.at[5])
    tbl_copy.start()

    with jax.named_scope("norm_z_wait"):
        wait_bytes(all_but_one(norm_z), recv("n", 0))
    acc = jnp.sum(norm_z[...], axis=0)
    norm_s[1] = acc
    norm_y[q] = acc
    for d in range(1, n_mp):
        send(norm_s.at[1], norm_y.at[q], recv("n", 1), f, rot(q, d, n_mp))
    tbl_copy.wait()
    p_exchange(0, 0)
    with jax.named_scope("norm_y_wait"):
        wait_bytes(all_but_one(norm_y), recv("n", 1))
    acc = jnp.sum(norm_y[...], axis=0)
    norm_s[2] = acc
    norm_x[me] = acc
    for dx, dc in near:
        send(
            norm_s.at[2],
            norm_x.at[me],
            recv("n", 2),
            fid(rot(x, dx, NX), z, rot(c, dc, NC)),
        )
    p_exchange(0, 1)
    f_spread()
    with jax.named_scope("norm_x_wait"):
        wait_bytes(all_but_one(norm_x), recv("n", 2))
    acc = jnp.sum(norm_x[...], axis=0)
    norm_sum = jnp.sum(jnp.sum(acc, axis=0, keepdims=True), axis=1, keepdims=True)
    clip = jnp.minimum(1.0, CLIP_RMS * (float(n_entries) ** 0.5) / jnp.sqrt(norm_sum))

    loads[1].wait()
    for r in range(CHUNKS):
        rows = slice(r * RC, (r + 1) * RC)
        nxt = FIRST_DECAY * f_v[rows, :] + ((1.0 - FIRST_DECAY) * clip) * g_v[rows, :].astype(F32)
        f_v[rows, :] = nxt
        low = nxt.astype(BF16)
        if r < FOLD:
            p_spread(1, r, low)
        else:
            for j in range(COLBLK):
                ms[r - FOLD, j] = low[:, j * BLOCK : (j + 1) * BLOCK]
            m_spread(r - FOLD)
    wait_units(1024, in_sem.at[2])
    qlt_v[...] = ql_v[...].reshape(BLOCK, BLOCK).T
    qrt_v[...] = qr_v[...].T
    f_exchange()
    p_exchange(1, 0)
    p_exchange(1, 1)
    p_gather(0, 0)
    m_exchange(0)
    p_gather(0, 1)
    f_gather()
    m_exchange(1)

    for r in range(FOLD):
        p_assemble(0, r)
    f_assemble()
    with jax.named_scope("owner_gradient"):
        live = tbl[2, f] > 0
        block = blk[0].reshape(BLOCK, BLOCK)
        half = mm(qlt_v[...], block).astype(BF16)
        rotated = clip * mm(half, qr_v[...])
        second = SECOND_DECAY * sm_v[...] + SECOND_RATE * rotated * rotated
        den_v[...] = jnp.sqrt(second) + EPSILON
        sm_v[...] = jnp.where(live, second, sm_v[...])
        scale = GRAM_RATE * clip * clip / BLOCK
        block_t = block.T
        lg_v[...] = jnp.where(live, GRAM_DECAY * lg_v[...] + scale * mm(block, block_t), lg_v[...])
        rg_v[...] = jnp.where(live, GRAM_DECAY * rg_v[...] + scale * mm(block_t, block), rg_v[...])

    for r in range(FOLD):
        p_gather(1, r)
    for r in range(FOLD):
        p_assemble(1, r)
    for r in range(CHUNKS - FOLD):
        m_assemble(r)
    with jax.named_scope("owner_moment"):
        mhalf = mm(qlt_v[...], blk[1].reshape(BLOCK, BLOCK)).astype(BF16)
        normed = (mm(mhalf, qr_v[...]) / den_v[...]).astype(BF16)

    def update(r):
        rows = ql_v[:, r * RC : (r + 1) * RC, :].reshape(HALF * NC * RC, BLOCK)
        return mm(mm(rows, normed).astype(BF16), qrt_v[...]).astype(BF16)

    group[0] = 1
    d_exchange(0, update(0))
    uf_spread([update(FOLD), update(FOLD + 1)])
    upd = update(1)

    wait_units(sent[0], send_sem.at[0])

    uf_exchange()
    u_spread(1, upd)
    d_gather(0)
    with jax.named_scope("uf_sent_wait"):
        wait_units(sent[2], send_sem.at[2])
    u_exchange(1)
    uf_gather()
    uf_swap()
    u_gather(1)
    d_finish(0)
    u_finish(1)
    uf_finish()
    wait_units(sent[1], send_sem.at[1])


def write_out(*refs):
    n = (len(refs) - 1) // 2
    copies = [
        pltpu.make_async_copy(refs[i], refs[n + i], refs[-1].at[i]) for i in range(n)
    ]
    for copy in copies:
        copy.start()
    for copy in copies:
        copy.wait()


def shards(
    gradient,
    first_moment,
    left_gram,
    right_gram,
    left_basis,
    right_basis,
    second_moment,
    block_target,
):
    rows, cols = gradient.shape
    n_fsdp = lax.axis_size("fsdp")
    n_mp = lax.axis_size("mp")
    n_blocks = block_target.shape[1]
    any_spec = pl.BlockSpec(memory_space=pl.ANY)
    vmem_spec = pl.BlockSpec(memory_space=pltpu.VMEM)
    vm = pltpu.VMEM
    dma = pltpu.SemaphoreType.DMA
    mat = (BLOCK, BLOCK)
    piece = (RC, LANE)
    strip = (RC, BLOCK)

    def per_chunk(n, *shape):
        return [vm(shape, BF16) for _ in range(n)]

    shapes = [((rows, cols), BF16), ((rows, cols), F32)] + [(mat, F32)] * 3
    held = pl.pallas_call(
        functools.partial(kernel, rows * cols * n_fsdp * n_mp),
        out_shape=tuple(vm(s, d) for s, d in shapes),
        in_specs=[any_spec] * 8,
        out_specs=(vmem_spec,) * 5,
        scratch_shapes=[
            vm((rows, cols), BF16),
            vm((HALF * NC, ROWS, BLOCK), BF16),
            vm(mat, BF16),
            vm(mat, BF16),
            vm(mat, BF16),
            vm(mat, F32),
            vm((3, 8, 128), F32),
            vm((n_mp, 8, 128), F32),
            vm((SLOTS, 8, 128), F32),
            vm((NZ, 8, 128), F32),
            vm((2, FOLD, NX, COLBLK) + piece, BF16),
            [per_chunk(FOLD, NX, COLBLK, *piece) for _ in range(2)],
            vm((2, FOLD, NZ, SLOTS) + piece, BF16),
            [per_chunk(FOLD, NZ, SLOTS, *piece) for _ in range(2)],
            vm((2, FOLD, SLOTS, HALF) + piece, BF16),
            vm((2, FOLD, NX, NC, HALF) + piece, BF16),
            vm((RC, cols), BF16),
            vm((NX, 2, COLBLK) + piece, BF16),
            vm((2 * LOCAL,) + piece, BF16),
            vm((NZ, SLOTS) + piece, BF16),
            vm((NZ, SLOTS) + piece, BF16),
            vm((NX, NC, NZ) + piece, BF16),
            vm((2, HALF * NC, ROWS, BLOCK), BF16),
            vm((CHUNKS - FOLD, COLBLK) + strip, BF16),
            per_chunk(CHUNKS - FOLD, NX, COLBLK, *strip),
            vm((CHUNKS - FOLD, NZ * NC) + strip, BF16),
            per_chunk(CHUNKS - FOLD, NZ * NC, *strip),
            vm((DIRECT, HALF, NC) + strip, BF16),
            per_chunk(DIRECT, NZ * NC, *strip),
            vm((DIRECT, NX, COLBLK) + strip, BF16),
            per_chunk(DIRECT, NX, COLBLK, *strip),
            vm((NX, NC, NZ) + piece, BF16),
            vm((SLOTS, NZ) + piece, BF16),
            vm((NZ, SLOTS) + piece, BF16),
            vm((NX, 2, COLBLK) + piece, BF16),
            vm((NX, 2, COLBLK) + piece, BF16),
            vm((RC, cols), BF16),
            vm((RC, cols), BF16),
            vm((CHUNKS, NX, NC, HALF) + piece, BF16),
            vm((CHUNKS, SLOTS, HALF) + piece, BF16),
            per_chunk(CHUNKS, NZ, SLOTS, *piece),
            vm((CHUNKS, NX, COLBLK) + piece, BF16),
            vm((CHUNKS, NX, COLBLK) + piece, BF16),
            pltpu.SMEM((1, n_blocks), jnp.int32),
            vm((1, n_blocks), jnp.int32),
            vm((8, 128), jnp.int32),
            pltpu.SMEM((8, 128), jnp.int32),
            vm((1024, RC, LANE), BF16),
            dma((6,)),
            dma((3,)),
            dma((len(RECV),)),
        ],
        compiler_params=pltpu.CompilerParams(
            collective_id=0, has_side_effects=True, vmem_limit_bytes=59 * 2**20
        ),
        cost_estimate=pl.CostEstimate(
            flops=16 * BLOCK**3, bytes_accessed=12 * 2**20, transcendentals=BLOCK**2
        ),
    )(
        block_target,
        gradient,
        first_moment,
        left_gram[0, 0],
        right_gram[0, 0],
        left_basis[0, 0].reshape(HALF * NC, ROWS, BLOCK),
        right_basis[0, 0],
        second_moment[0, 0],
    )
    out = pl.pallas_call(
        write_out,
        out_shape=tuple(jax.ShapeDtypeStruct(s, d) for s, d in shapes),
        in_specs=[vmem_spec] * 5,
        out_specs=(any_spec,) * 5,
        scratch_shapes=[dma((5,))],
        compiler_params=pltpu.CompilerParams(vmem_limit_bytes=2**20),
    )(*held)
    return (out[0], out[1]) + tuple(o[None, None] for o in out[2:])


def solution(mesh):
    return jax.shard_map(
        shards,
        mesh=mesh,
        in_specs=(
            P("fsdp", "mp"),
            P("fsdp", "mp"),
            P("fsdp", "mp", None, None),
            P("fsdp", "mp", None, None),
            P("fsdp", "mp", None, None),
            P("fsdp", "mp", None, None),
            P("fsdp", "mp", None, None),
            P("mp", None),
        ),
        out_specs=(
            P("fsdp", "mp"),
            P("fsdp", "mp"),
            P("fsdp", "mp", None, None),
            P("fsdp", "mp", None, None),
            P("fsdp", "mp", None, None),
        ),
        check_vma=False,
    )
```

```python
import functools
import math

import jax
import jax.numpy as jnp
from jax import lax
from jax.experimental import pallas as pl
from jax.experimental.pallas import tpu as pltpu
from jax.sharding import PartitionSpec as P

CLIP_RMS = 0.5
FIRST_DECAY = 0.9
GRAM_DECAY = 0.95
GRAM_RATE = 0.05
SECOND_DECAY = 0.95
SECOND_RATE = 0.05
EPSILON = 1e-08

MESH = pl.DeviceIdType.MESH
NX, NZ, NC = 4, 8, 2
HALF = NZ // 2
COLBLK = 7
SLOTS = NX * NC
LOCAL = NX * COLBLK
ROWS = 64
BLOCK = 512
LANE = BLOCK // NX
CHUNKS = 4
FOLD = 2
DIRECT = 1
RC = ROWS // CHUNKS
Z_ORDER = (4, 5, 3, 6, 2, 7, 1)
X_ORDER = (2, 1, 3)

UNIT = RC * LANE * 2
PLAIN = [(a, r) for a in range(2) for r in range(FOLD)]
LATER = [(1, r) for r in range(FOLD, CHUNKS)] + [(2, 0), (2, 1)]
RECV = [(k,) + ar for k in "xz" for ar in PLAIN + LATER]
RECV += [("g",) + ar for ar in PLAIN + [(2, 1)]]
RECV += [("f", i) for i in range(9) if i != 6] + [("s", d) for d in X_ORDER] + [("n", i) for i in range(3)]

BF16, F32 = jnp.bfloat16, jnp.float32


def mm(a, b):
    return jnp.dot(a, b, preferred_element_type=F32)


def kernel(
    n_entries,
    tgt_hbm,
    grad_hbm,
    first_hbm,
    lg_hbm,
    rg_hbm,
    ql_hbm,
    qr_hbm,
    sm_hbm,
    out_v,
    f_v,
    lg_v,
    rg_v,
    sm_v,
    g_v,
    ql_v,
    qr_v,
    qlt_v,
    qrt_v,
    den_v,
    norm_s,
    norm_y,
    norm_x,
    norm_z,
    xs,
    xr,
    zs,
    zr,
    gs,
    gr,
    fx,
    fs,
    fr,
    fzs,
    fz,
    fg,
    blk,
    ms,
    mx,
    mzs,
    mz,
    uds,
    udz,
    udp,
    udx,
    fub,
    fug,
    fuz,
    fus,
    fuf,
    fsr,
    ub,
    ug,
    uz,
    us,
    uf,
    tgt_s,
    tgt_v,
    tbl_v,
    tbl,
    units,
    in_sem,
    send_sem,
    recv_sem,
):
    f = lax.axis_index("fsdp")
    q = lax.axis_index("mp")
    c = lax.rem(f, NC)
    z = lax.rem(f // NC, NZ)
    x = f // (NC * NZ)
    side_here = z // HALF
    n_mp = lax.axis_size("mp")

    def fid(xx, zz, cc):
        return (xx * NZ + zz) * NC + cc

    def rot(v, d, n):
        return lax.rem(v + d, n)

    near = [(dx, dc) for dx in X_ORDER + (0,) for dc in range(NC) if dx or dc]
    barrier = pltpu.get_barrier_semaphore()
    peers = [(fid(x, rot(z, d, NZ), rot(c, dc, NC)), q) for d in Z_ORDER for dc in range(NC)]
    peers += [(fid(rot(x, dx, NX), z, rot(c, dc, NC)), q) for dx, dc in near]
    peers += [(f, rot(q, d, n_mp)) for d in range(1, n_mp)]
    for peer in peers:
        pl.semaphore_signal(barrier, inc=1, device_id=peer, device_id_type=MESH)

    tgt_loads = [
        pltpu.make_async_copy(tgt_hbm, tgt_s, in_sem.at[3]),
        pltpu.make_async_copy(tgt_hbm, tgt_v, in_sem.at[4]),
    ]
    loads = [
        pltpu.make_async_copy(src, dst, in_sem.at[min(i, 2)])
        for i, (src, dst) in enumerate(
            (
                (grad_hbm, g_v),
                (first_hbm, f_v),
                (ql_hbm, ql_v),
                (qr_hbm, qr_v),
                (sm_hbm, sm_v),
                (lg_hbm, lg_v),
                (rg_hbm, rg_v),
            )
        )
    ]
    for load in loads[:1] + tgt_loads + loads[1:]:
        load.start()

    loads[0].wait()
    wide = g_v[...].astype(F32)
    cols = jnp.sum((wide * wide).reshape(ROWS // 8, 8, wide.shape[1]), axis=0)
    acc = cols[:, :128]
    for i in range(1, cols.shape[1] // 128):
        acc = acc + cols[:, i * 128 : (i + 1) * 128]
    norm_s[0] = acc
    norm_z[z] = acc

    with jax.named_scope("barrier"):
        pl.semaphore_wait(barrier, len(peers))

    sent = [0, 0, 0]
    group = [0]

    def send(src, dst, rsem, pf, pq=q, under=None):
        under = group[0] if under is None else under
        sent[under] += math.prod(src.shape) * src.dtype.itemsize // UNIT
        pltpu.make_async_remote_copy(
            src_ref=src,
            dst_ref=dst,
            send_sem=send_sem.at[under],
            recv_sem=rsem,
            device_id=(pf, pq),
            device_id_type=MESH,
        ).start()

    def recv(*key):
        return recv_sem.at[RECV.index(key)]

    def wait_units(n, sem):
        wait_bytes(units.at[pl.ds(0, n)], sem)

    def wait_bytes(ref, sem):
        pltpu.make_async_copy(ref, ref, sem).wait()

    def some(ref, n):
        return ref.at[pl.ds(0, n)]

    def all_but_one(ref):
        return some(ref, ref.shape[0] - 1)

    def p_spread(a, r, rows):
        for xx in range(NX):
            for j in range(COLBLK):
                lo = j * BLOCK + xx * LANE
                xs[a, r, xx, j] = rows[:, lo : lo + LANE]
        for d in X_ORDER:
            px = rot(x, d, NX)
            send(xs.at[a, r, px], xr[a][r].at[x], recv("x", a, r), fid(px, z, c))
        xr[a][r][x] = xs[a, r, x]

    def p_exchange(a, r):
        with jax.named_scope("p_spread_wait"):
            wait_bytes(all_but_one(xr[a][r]), recv("x", a, r))

        def slots(pz, dst):
            for s in range(SLOTS):
                l = tbl[0, fid(s // NC, pz, s % NC)]
                dst[s] = xr[a][r][l // COLBLK, lax.rem(l, COLBLK)]

        for d in Z_ORDER:
            pz = rot(z, d, NZ)
            slots(pz, zs.at[a, r, pz])
            send(zs.at[a, r, pz], zr[a][r].at[z], recv("z", a, r), fid(x, pz, c))
        slots(z, zr[a][r].at[z])

    def p_gather(a, r):
        with jax.named_scope("p_exchange_wait"):
            wait_bytes(all_but_one(zr[a][r]), recv("z", a, r))
        for s in range(SLOTS):
            h = tbl[1, fid(s // NC, z, s % NC)]
            for i in range(HALF):
                gs[a, r, s, i] = zr[a][r][h * HALF + i, s]
        for dx, dc in near:
            px, pc = rot(x, dx, NX), rot(c, dc, NC)
            send(
                gs.at[a, r, px * NC + pc],
                gr.at[a, r, x, c],
                recv("g", a, r),
                fid(px, z, pc),
            )
        gr[a, r, x, c] = gs[a, r, x * NC + c]

    def p_assemble(a, r):
        with jax.named_scope("p_gather_wait"):
            wait_bytes(all_but_one(gs.at[a, r]), recv("g", a, r))
        for xx in range(NX):
            for cc in range(NC):
                for i in range(HALF):
                    blk[a, i * NC + cc, r * RC : (r + 1) * RC, xx * LANE : (xx + 1) * LANE] = gr[
                        a, r, xx, cc, i
                    ]

    mate = fid(x, rot(z, HALF, NZ), c)

    def f_swap():
        src = g_v.at[pl.ds(pl.multiple_of((FOLD + 1 - side_here) * RC, RC), RC), :]
        send(src, fx, recv("f", 0), mate)

    def f_spread():
        with jax.named_scope("f_swap_wait"):
            wait_bytes(fx, recv("f", 0))
        mine = g_v[pl.ds(pl.multiple_of((FOLD + side_here) * RC, RC), RC), :]
        theirs = fx[...]
        for xx in range(NX):
            for j in range(COLBLK):
                lo = j * BLOCK + xx * LANE
                fs[xx, side_here, j] = mine[:, lo : lo + LANE]
                fs[xx, 1 - side_here, j] = theirs[:, lo : lo + LANE]
        for d in X_ORDER:
            px = rot(x, d, NX)
            for h in range(2):
                send(
                    fs.at[px, h],
                    fr.at[pl.ds((x * 2 + h) * COLBLK, COLBLK)],
                    recv("f", 1),
                    fid(px, z, c),
                )
        for h in range(2):
            fr[pl.ds((x * 2 + h) * COLBLK, COLBLK)] = fs[x, h]

    def f_exchange():
        with jax.named_scope("f_spread_wait"):
            wait_bytes(some(fr, 2 * COLBLK * (NX - 1)), recv("f", 1))

        def slots(pz, dst):
            for s in range(SLOTS):
                dst[s] = fr[tbl[3, fid(s // NC, pz, s % NC)]]

        for d in Z_ORDER:
            pz = rot(z, d, NZ)
            slots(pz, fzs.at[pz])
            send(fzs.at[pz], fz.at[z], recv("f", 2), fid(x, pz, c))
        slots(z, fz.at[z])

    def f_gather():
        with jax.named_scope("f_exchange_wait"):
            wait_bytes(all_but_one(fz), recv("f", 2))
        for dx, dc in near:
            px, pc = rot(x, dx, NX), rot(c, dc, NC)
            send(fz.at[:, px * NC + pc], fg.at[x, c], recv("f", 3), fid(px, z, pc))
        for i in range(NZ):
            fg[x, c, i] = fz[i, x * NC + c]

    def f_assemble():
        with jax.named_scope("f_gather_wait"):
            wait_bytes(some(fz, NZ - 1), recv("f", 3))
        for xx in range(NX):
            for cc in range(NC):
                for i in range(NZ):
                    lo = (FOLD + i // HALF) * RC
                    blk[0, i % HALF * NC + cc, lo : lo + RC, xx * LANE : (xx + 1) * LANE] = fg[
                        xx, cc, i
                    ]

    def m_spread(r):
        for d in X_ORDER:
            send(ms.at[r], mx[r].at[x], recv("x", 1, FOLD + r), fid(rot(x, d, NX), z, c))
        mx[r][x] = ms[r]

    def m_exchange(r):
        with jax.named_scope("m_spread_wait"):
            wait_bytes(all_but_one(mx[r]), recv("x", 1, FOLD + r))

        def slot(pz, pc, dst):
            l = tbl[0, fid(x, pz, pc)]
            dst[...] = mx[r][l // COLBLK, lax.rem(l, COLBLK)]

        for d in Z_ORDER + (0,):
            pz = rot(z, d, NZ)
            for dc in range(NC):
                pc = rot(c, dc, NC)
                if d or dc:
                    slot(pz, pc, mzs.at[r, pz * NC + pc])
                    send(
                        mzs.at[r, pz * NC + pc],
                        mz[r].at[z * NC + c],
                        recv("z", 1, FOLD + r),
                        fid(x, pz, pc),
                    )
        slot(z, c, mz[r].at[z * NC + c])


    def m_assemble(r):
        with jax.named_scope("m_exchange_wait"):
            wait_bytes(all_but_one(mz[r]), recv("z", 1, FOLD + r))
        h = tbl[1, f]
        for i in range(HALF):
            for cc in range(NC):
                lo = (FOLD + r) * RC
                blk[1, i * NC + cc, lo : lo + RC, :] = mz[r][(h * HALF + i) * NC + cc]

    def d_exchange(r, upd):
        for i in range(HALF):
            for cc in range(NC):
                lo = (i * NC + cc) * RC
                uds[r, i, cc] = upd[lo : lo + RC, :]
        for d in Z_ORDER + (0,):
            pz = rot(z, d, NZ)
            for dc in range(NC):
                pc = rot(c, dc, NC)
                if d or dc:
                    send(
                        uds.at[r, lax.rem(pz, HALF), pc],
                        udz[r].at[z * NC + c],
                        recv("z", 2, r),
                        fid(x, pz, pc),
                    )
        udz[r][z * NC + c] = uds[r, lax.rem(z, HALF), c]

    def d_gather(r):
        with jax.named_scope("d_exchange_wait"):
            wait_bytes(all_but_one(udz[r]), recv("z", 2, r))
        for d in X_ORDER + (0,):
            px = rot(x, d, NX)
            for j in range(COLBLK):
                t = tgt_s[0, (px * 2 + side_here) * COLBLK + j]
                part = udz[r][lax.rem(t, NZ * NC)]
                if d:
                    udp[r, px, j] = part
                else:
                    udx[r][x, j] = part
            if d:
                send(udp.at[r, px], udx[r].at[x], recv("x", 2, r), fid(px, z, c))

    def d_finish(r):
        with jax.named_scope("d_gather_wait"):
            wait_bytes(all_but_one(udx[r]), recv("x", 2, r))
        for j in range(COLBLK):
            t = tgt_s[0, (x * 2 + side_here) * COLBLK + j]
            out_v[r * RC : (r + 1) * RC, j * BLOCK : (j + 1) * BLOCK] = udx[r][t // (NZ * NC), j]

    me = x * NC + c

    def u_spread(r, upd):
        for xx in range(NX):
            for cc in range(NC):
                for i in range(HALF):
                    lo = (i * NC + cc) * RC
                    ub[r, xx, cc, i] = upd[lo : lo + RC, xx * LANE : (xx + 1) * LANE]
        for dx, dc in near:
            px, pc = rot(x, dx, NX), rot(c, dc, NC)
            send(ub.at[r, px, pc], ug.at[r, me], recv("g", 2, r), fid(px, z, pc))
        ug[r, me] = ub[r, x, c]

    def u_exchange(r):
        with jax.named_scope("u_spread_wait"):
            wait_bytes(all_but_one(ug.at[r]), recv("g", 2, r))
        for d in Z_ORDER:
            pz = rot(z, d, NZ)
            send(
                ug.at[r, :, lax.rem(pz, HALF)],
                uz[r].at[z],
                recv("z", 2, r),
                fid(x, pz, c),
            )
        for s in range(SLOTS):
            uz[r][z, s] = ug[r, s, lax.rem(z, HALF)]

    def u_gather(r):
        with jax.named_scope("u_exchange_wait"):
            wait_bytes(all_but_one(uz[r]), recv("z", 2, r))
        for d in X_ORDER + (0,):
            px = rot(x, d, NX)
            for j in range(COLBLK):
                t = tgt_s[0, (px * 2 + side_here) * COLBLK + j]
                slot = (t // (NC * NZ)) * NC + lax.rem(t, NC)
                part = uz[r][lax.rem(t // NC, NZ), slot]
                if d:
                    us[r, px, j] = part
                else:
                    uf[r, x, j] = part
            if d:
                send(us.at[r, px], uf.at[r, x], recv("x", 2, r), fid(px, z, c))

    def u_finish(r):
        with jax.named_scope("u_gather_wait"):
            wait_bytes(all_but_one(uf.at[r]), recv("x", 2, r))
        for xx in range(NX):
            for j in range(COLBLK):
                lo = j * BLOCK + xx * LANE
                out_v[r * RC : (r + 1) * RC, lo : lo + LANE] = uf[r, xx, j]

    def uf_spread(upds):
        for h in range(2):
            for xx in range(NX):
                for cc in range(NC):
                    for i in range(HALF):
                        lo = (i * NC + cc) * RC
                        fub[xx, cc, h * HALF + i] = upds[h][
                            lo : lo + RC, xx * LANE : (xx + 1) * LANE
                        ]
        for dx, dc in near:
            px, pc = rot(x, dx, NX), rot(c, dc, NC)
            send(fub.at[px, pc], fug.at[me], recv("f", 4), fid(px, z, pc))
        fug[me] = fub[x, c]

    def uf_exchange():
        with jax.named_scope("uf_spread_wait"):
            wait_bytes(all_but_one(fug), recv("f", 4))
        for d in Z_ORDER:
            pz = rot(z, d, NZ)
            send(fug.at[:, pz], fuz.at[z], recv("f", 5), fid(x, pz, c), under=2)
        for s in range(SLOTS):
            fuz[z, s] = fug[s, z]

    def uf_gather():
        with jax.named_scope("uf_exchange_wait"):
            wait_bytes(all_but_one(fuz), recv("f", 5))
        for i, h in enumerate((1 - side_here, side_here)):
            for d in X_ORDER + (0,):
                px = rot(x, d, NX)
                for j in range(COLBLK):
                    t = tgt_s[0, (px * 2 + h) * COLBLK + j]
                    slot = (t // (NC * NZ)) * NC + lax.rem(t, NC)
                    part = fuz[lax.rem(t // NC, NZ), slot]
                    if d:
                        fus[h, px, j] = part
                    else:
                        fuf[h, x, j] = part
                if d:
                    send(
                        fus.at[h, px],
                        fuf.at[h, x],
                        recv("s", d) if i == 0 else recv("f", 8),
                        fid(px, z, c),
                    )

    def uf_swap():
        for d in (0,) + X_ORDER[1:] + X_ORDER[:1]:
            xx = rot(x, NX - d, NX)
            piece = fuf.at[1 - side_here, xx]
            if d:
                with jax.named_scope("uf_gather_wait"):
                    wait_bytes(piece, recv("s", d))
            send(piece, fsr.at[xx], recv("f", 7), mate)

    def uf_keep():
        wait_bytes(some(fuf.at[0], NX - 1), recv("f", 8))
        rows = pl.ds(pl.multiple_of((FOLD + side_here) * RC, RC), RC)
        for xx in range(NX):
            for j in range(COLBLK):
                lo = j * BLOCK + xx * LANE
                out_v[rows, lo : lo + LANE] = fuf[side_here, xx, j]

    def uf_finish():
        with jax.named_scope("uf_swap_wait"):
            wait_bytes(fsr, recv("f", 7))
        rows = pl.ds(pl.multiple_of((FOLD + 1 - side_here) * RC, RC), RC)
        for xx in range(NX):
            for j in range(COLBLK):
                lo = j * BLOCK + xx * LANE
                out_v[rows, lo : lo + LANE] = fsr[xx, j]

    for d in Z_ORDER:
        send(norm_s.at[0], norm_z.at[z], recv("n", 0), fid(x, rot(z, d, NZ), c))
    p_spread(0, 0, g_v[:RC, :])
    f_swap()
    p_spread(0, 1, g_v[RC : 2 * RC, :])

    for load in tgt_loads:
        load.wait()
    n_blocks = tgt_v.shape[1]
    sub = lax.broadcasted_iota(jnp.int32, (n_blocks, 128), 0)
    lane = lax.broadcasted_iota(jnp.int32, (n_blocks, 128), 1)
    sub_sq = lax.broadcasted_iota(jnp.int32, (n_blocks, n_blocks), 0)
    lane_sq = lax.broadcasted_iota(jnp.int32, (n_blocks, n_blocks), 1)
    diag = jnp.where(sub_sq == lane_sq, jnp.broadcast_to(tgt_v[...], sub_sq.shape), 0)
    named = jnp.sum(diag, axis=1, keepdims=True) == lane
    band = sub // COLBLK
    side = lax.rem(band, 2)
    local = jnp.where(side == side_here, sub - (band - band // 2) * COLBLK, 0)
    for i, code in enumerate((local, side, jnp.ones_like(sub), sub)):
        tbl_v[i : i + 1, :] = jnp.max(jnp.where(named, code, 0), axis=0, keepdims=True)
    tbl_copy = pltpu.make_async_copy(tbl_v, tbl, in_sem.at[5])
    tbl_copy.start()

    with jax.named_scope("norm_z_wait"):
        wait_bytes(all_but_one(norm_z), recv("n", 0))
    acc = jnp.sum(norm_z[...], axis=0)
    norm_s[1] = acc
    norm_y[q] = acc
    for d in range(1, n_mp):
        send(norm_s.at[1], norm_y.at[q], recv("n", 1), f, rot(q, d, n_mp))
    tbl_copy.wait()
    p_exchange(0, 0)
    with jax.named_scope("norm_y_wait"):
        wait_bytes(all_but_one(norm_y), recv("n", 1))
    acc = jnp.sum(norm_y[...], axis=0)
    norm_s[2] = acc
    norm_x[me] = acc
    for dx, dc in near:
        send(
            norm_s.at[2],
            norm_x.at[me],
            recv("n", 2),
            fid(rot(x, dx, NX), z, rot(c, dc, NC)),
        )
    p_exchange(0, 1)
    f_spread()
    with jax.named_scope("norm_x_wait"):
        wait_bytes(all_but_one(norm_x), recv("n", 2))
    acc = jnp.sum(norm_x[...], axis=0)
    norm_sum = jnp.sum(jnp.sum(acc, axis=0, keepdims=True), axis=1, keepdims=True)
    clip = jnp.minimum(1.0, CLIP_RMS * (float(n_entries) ** 0.5) / jnp.sqrt(norm_sum))

    loads[1].wait()
    for r in range(CHUNKS):
        rows = slice(r * RC, (r + 1) * RC)
        nxt = FIRST_DECAY * f_v[rows, :] + ((1.0 - FIRST_DECAY) * clip) * g_v[rows, :].astype(F32)
        f_v[rows, :] = nxt
        low = nxt.astype(BF16)
        if r < FOLD:
            p_spread(1, r, low)
        else:
            for j in range(COLBLK):
                ms[r - FOLD, j] = low[:, j * BLOCK : (j + 1) * BLOCK]
            m_spread(r - FOLD)
    wait_units(1024, in_sem.at[2])
    qlt_v[...] = ql_v[...].reshape(BLOCK, BLOCK).T
    qrt_v[...] = qr_v[...].T
    f_exchange()
    p_exchange(1, 0)
    p_exchange(1, 1)
    p_gather(0, 0)
    m_exchange(0)
    p_gather(0, 1)
    f_gather()
    m_exchange(1)

    for r in range(FOLD):
        p_assemble(0, r)
    f_assemble()
    with jax.named_scope("owner_gradient"):
        live = tbl[2, f] > 0
        block = blk[0].reshape(BLOCK, BLOCK)
        half = mm(qlt_v[...], block).astype(BF16)
        rotated = clip * mm(half, qr_v[...])
        second = SECOND_DECAY * sm_v[...] + SECOND_RATE * rotated * rotated
        den_v[...] = jnp.sqrt(second) + EPSILON
        sm_v[...] = jnp.where(live, second, sm_v[...])
        scale = GRAM_RATE * clip * clip / BLOCK
        block_t = block.T
        lg_v[...] = jnp.where(live, GRAM_DECAY * lg_v[...] + scale * mm(block, block_t), lg_v[...])
        rg_v[...] = jnp.where(live, GRAM_DECAY * rg_v[...] + scale * mm(block_t, block), rg_v[...])

    for r in range(FOLD):
        p_gather(1, r)
    for r in range(FOLD):
        p_assemble(1, r)
    for r in range(CHUNKS - FOLD):
        m_assemble(r)
    with jax.named_scope("owner_moment"):
        mhalf = mm(qlt_v[...], blk[1].reshape(BLOCK, BLOCK)).astype(BF16)
        normed = (mm(mhalf, qr_v[...]) / den_v[...]).astype(BF16)

    def update(r):
        rows = ql_v[:, r * RC : (r + 1) * RC, :].reshape(HALF * NC * RC, BLOCK)
        return mm(mm(rows, normed).astype(BF16), qrt_v[...]).astype(BF16)

    group[0] = 1
    d_exchange(0, update(0))
    uf_spread([update(FOLD), update(FOLD + 1)])
    upd = update(1)

    wait_units(sent[0], send_sem.at[0])

    uf_exchange()
    u_spread(1, upd)
    d_gather(0)
    with jax.named_scope("uf_sent_wait"):
        wait_units(sent[2], send_sem.at[2])
    u_exchange(1)
    uf_gather()
    uf_swap()
    u_gather(1)
    uf_keep()
    d_finish(0)
    u_finish(1)
    uf_finish()
    wait_units(sent[1], send_sem.at[1])


def write_out(*refs):
    n = (len(refs) - 1) // 2
    copies = [
        pltpu.make_async_copy(refs[i], refs[n + i], refs[-1].at[i]) for i in range(n)
    ]
    for copy in copies:
        copy.start()
    for copy in copies:
        copy.wait()


def shards(
    gradient,
    first_moment,
    left_gram,
    right_gram,
    left_basis,
    right_basis,
    second_moment,
    block_target,
):
    rows, cols = gradient.shape
    n_fsdp = lax.axis_size("fsdp")
    n_mp = lax.axis_size("mp")
    n_blocks = block_target.shape[1]
    any_spec = pl.BlockSpec(memory_space=pl.ANY)
    vmem_spec = pl.BlockSpec(memory_space=pltpu.VMEM)
    vm = pltpu.VMEM
    dma = pltpu.SemaphoreType.DMA
    mat = (BLOCK, BLOCK)
    piece = (RC, LANE)
    strip = (RC, BLOCK)

    def per_chunk(n, *shape):
        return [vm(shape, BF16) for _ in range(n)]

    shapes = [((rows, cols), BF16), ((rows, cols), F32)] + [(mat, F32)] * 3
    held = pl.pallas_call(
        functools.partial(kernel, rows * cols * n_fsdp * n_mp),
        out_shape=tuple(vm(s, d) for s, d in shapes),
        in_specs=[any_spec] * 8,
        out_specs=(vmem_spec,) * 5,
        scratch_shapes=[
            vm((rows, cols), BF16),
            vm((HALF * NC, ROWS, BLOCK), BF16),
            vm(mat, BF16),
            vm(mat, BF16),
            vm(mat, BF16),
            vm(mat, F32),
            vm((3, 8, 128), F32),
            vm((n_mp, 8, 128), F32),
            vm((SLOTS, 8, 128), F32),
            vm((NZ, 8, 128), F32),
            vm((2, FOLD, NX, COLBLK) + piece, BF16),
            [per_chunk(FOLD, NX, COLBLK, *piece) for _ in range(2)],
            vm((2, FOLD, NZ, SLOTS) + piece, BF16),
            [per_chunk(FOLD, NZ, SLOTS, *piece) for _ in range(2)],
            vm((2, FOLD, SLOTS, HALF) + piece, BF16),
            vm((2, FOLD, NX, NC, HALF) + piece, BF16),
            vm((RC, cols), BF16),
            vm((NX, 2, COLBLK) + piece, BF16),
            vm((2 * LOCAL,) + piece, BF16),
            vm((NZ, SLOTS) + piece, BF16),
            vm((NZ, SLOTS) + piece, BF16),
            vm((NX, NC, NZ) + piece, BF16),
            vm((2, HALF * NC, ROWS, BLOCK), BF16),
            vm((CHUNKS - FOLD, COLBLK) + strip, BF16),
            per_chunk(CHUNKS - FOLD, NX, COLBLK, *strip),
            vm((CHUNKS - FOLD, NZ * NC) + strip, BF16),
            per_chunk(CHUNKS - FOLD, NZ * NC, *strip),
            vm((DIRECT, HALF, NC) + strip, BF16),
            per_chunk(DIRECT, NZ * NC, *strip),
            vm((DIRECT, NX, COLBLK) + strip, BF16),
            per_chunk(DIRECT, NX, COLBLK, *strip),
            vm((NX, NC, NZ) + piece, BF16),
            vm((SLOTS, NZ) + piece, BF16),
            vm((NZ, SLOTS) + piece, BF16),
            vm((2, NX, COLBLK) + piece, BF16),
            vm((2, NX, COLBLK) + piece, BF16),
            vm((NX, COLBLK) + piece, BF16),
            vm((CHUNKS, NX, NC, HALF) + piece, BF16),
            vm((CHUNKS, SLOTS, HALF) + piece, BF16),
            per_chunk(CHUNKS, NZ, SLOTS, *piece),
            vm((CHUNKS, NX, COLBLK) + piece, BF16),
            vm((CHUNKS, NX, COLBLK) + piece, BF16),
            pltpu.SMEM((1, n_blocks), jnp.int32),
            vm((1, n_blocks), jnp.int32),
            vm((8, 128), jnp.int32),
            pltpu.SMEM((8, 128), jnp.int32),
            vm((1024, RC, LANE), BF16),
            dma((6,)),
            dma((3,)),
            dma((len(RECV),)),
        ],
        compiler_params=pltpu.CompilerParams(
            collective_id=0, has_side_effects=True, vmem_limit_bytes=59 * 2**20
        ),
        cost_estimate=pl.CostEstimate(
            flops=16 * BLOCK**3, bytes_accessed=12 * 2**20, transcendentals=BLOCK**2
        ),
    )(
        block_target,
        gradient,
        first_moment,
        left_gram[0, 0],
        right_gram[0, 0],
        left_basis[0, 0].reshape(HALF * NC, ROWS, BLOCK),
        right_basis[0, 0],
        second_moment[0, 0],
    )
    out = pl.pallas_call(
        write_out,
        out_shape=tuple(jax.ShapeDtypeStruct(s, d) for s, d in shapes),
        in_specs=[vmem_spec] * 5,
        out_specs=(any_spec,) * 5,
        scratch_shapes=[dma((5,))],
        compiler_params=pltpu.CompilerParams(vmem_limit_bytes=2**20),
    )(*held)
    return (out[0], out[1]) + tuple(o[None, None] for o in out[2:])


def solution(mesh):
    return jax.shard_map(
        shards,
        mesh=mesh,
        in_specs=(
            P("fsdp", "mp"),
            P("fsdp", "mp"),
            P("fsdp", "mp", None, None),
            P("fsdp", "mp", None, None),
            P("fsdp", "mp", None, None),
            P("fsdp", "mp", None, None),
            P("fsdp", "mp", None, None),
            P("mp", None),
        ),
        out_specs=(
            P("fsdp", "mp"),
            P("fsdp", "mp"),
            P("fsdp", "mp", None, None),
            P("fsdp", "mp", None, None),
            P("fsdp", "mp", None, None),
        ),
        check_vma=False,
    )
```

```python
import functools
import math

import jax
import jax.numpy as jnp
from jax import lax
from jax.experimental import pallas as pl
from jax.experimental.pallas import tpu as pltpu
from jax.sharding import PartitionSpec as P

CLIP_RMS = 0.5
FIRST_DECAY = 0.9
GRAM_DECAY = 0.95
GRAM_RATE = 0.05
SECOND_DECAY = 0.95
SECOND_RATE = 0.05
EPSILON = 1e-08

MESH = pl.DeviceIdType.MESH
NX, NZ, NC = 4, 8, 2
HALF = NZ // 2
COLBLK = 7
SLOTS = NX * NC
LOCAL = NX * COLBLK
ROWS = 64
BLOCK = 512
LANE = BLOCK // NX
CHUNKS = 4
FOLD = 2
DIRECT = 1
RC = ROWS // CHUNKS
Z_ORDER = (4, 5, 3, 6, 2, 7, 1)
X_ORDER = (2, 1, 3)

UNIT = RC * LANE * 2
PLAIN = [(0, r) for r in range(FOLD)]
LATER = [(1, r) for r in range(FOLD, CHUNKS)] + [(2, 0), (2, 1)]
RECV = [(k,) + ar for k in "xz" for ar in PLAIN + LATER]
RECV += [("g",) + ar for ar in PLAIN + [(2, 1)]]
RECV += [("f", a, i) for a in range(2) for i in range(4)] + [("f", i) for i in (4, 5, 7, 8)] + [("s", d) for d in X_ORDER] + [("n", i) for i in range(3)]

BF16, F32 = jnp.bfloat16, jnp.float32


def mm(a, b):
    return jnp.dot(a, b, preferred_element_type=F32)


def kernel(
    n_entries,
    tgt_hbm,
    grad_hbm,
    first_hbm,
    lg_hbm,
    rg_hbm,
    ql_hbm,
    qr_hbm,
    sm_hbm,
    out_v,
    f_v,
    lg_v,
    rg_v,
    sm_v,
    g_v,
    ql_v,
    qr_v,
    qlt_v,
    qrt_v,
    den_v,
    norm_s,
    norm_y,
    norm_x,
    norm_z,
    xs,
    xr,
    zs,
    zr,
    gs,
    gr,
    mf,
    fx,
    fs,
    fr,
    fzs,
    fz,
    fg,
    blk,
    ms,
    mx,
    mzs,
    mz,
    uds,
    udz,
    udp,
    udx,
    fub,
    fug,
    fuz,
    fus,
    fuf,
    fsr,
    ub,
    ug,
    uz,
    us,
    uf,
    tgt_s,
    tgt_v,
    tbl_v,
    tbl,
    units,
    in_sem,
    send_sem,
    recv_sem,
):
    f = lax.axis_index("fsdp")
    q = lax.axis_index("mp")
    c = lax.rem(f, NC)
    z = lax.rem(f // NC, NZ)
    x = f // (NC * NZ)
    side_here = z // HALF
    n_mp = lax.axis_size("mp")

    def fid(xx, zz, cc):
        return (xx * NZ + zz) * NC + cc

    def rot(v, d, n):
        return lax.rem(v + d, n)

    near = [(dx, dc) for dx in X_ORDER + (0,) for dc in range(NC) if dx or dc]
    barrier = pltpu.get_barrier_semaphore()
    peers = [(fid(x, rot(z, d, NZ), rot(c, dc, NC)), q) for d in Z_ORDER for dc in range(NC)]
    peers += [(fid(rot(x, dx, NX), z, rot(c, dc, NC)), q) for dx, dc in near]
    peers += [(f, rot(q, d, n_mp)) for d in range(1, n_mp)]
    for peer in peers:
        pl.semaphore_signal(barrier, inc=1, device_id=peer, device_id_type=MESH)

    tgt_loads = [
        pltpu.make_async_copy(tgt_hbm, tgt_s, in_sem.at[3]),
        pltpu.make_async_copy(tgt_hbm, tgt_v, in_sem.at[4]),
    ]
    loads = [
        pltpu.make_async_copy(src, dst, in_sem.at[min(i, 2)])
        for i, (src, dst) in enumerate(
            (
                (grad_hbm, g_v),
                (first_hbm, f_v),
                (ql_hbm, ql_v),
                (qr_hbm, qr_v),
                (sm_hbm, sm_v),
                (lg_hbm, lg_v),
                (rg_hbm, rg_v),
            )
        )
    ]
    for load in loads[:1] + tgt_loads + loads[1:]:
        load.start()

    loads[0].wait()
    wide = g_v[...].astype(F32)
    cols = jnp.sum((wide * wide).reshape(ROWS // 8, 8, wide.shape[1]), axis=0)
    acc = cols[:, :128]
    for i in range(1, cols.shape[1] // 128):
        acc = acc + cols[:, i * 128 : (i + 1) * 128]
    norm_s[0] = acc
    norm_z[z] = acc

    with jax.named_scope("barrier"):
        pl.semaphore_wait(barrier, len(peers))

    sent = [0, 0, 0, 0]
    group = [0]

    def send(src, dst, rsem, pf, pq=q, under=None):
        under = group[0] if under is None else under
        sent[under] += math.prod(src.shape) * src.dtype.itemsize // UNIT
        pltpu.make_async_remote_copy(
            src_ref=src,
            dst_ref=dst,
            send_sem=send_sem.at[under],
            recv_sem=rsem,
            device_id=(pf, pq),
            device_id_type=MESH,
        ).start()

    def recv(*key):
        return recv_sem.at[RECV.index(key)]

    def wait_units(n, sem):
        wait_bytes(units.at[pl.ds(0, n)], sem)

    def wait_bytes(ref, sem):
        pltpu.make_async_copy(ref, ref, sem).wait()

    def some(ref, n):
        return ref.at[pl.ds(0, n)]

    def all_but_one(ref):
        return some(ref, ref.shape[0] - 1)

    def p_spread(r, rows):
        for xx in range(NX):
            for j in range(COLBLK):
                lo = j * BLOCK + xx * LANE
                xs[r, xx, j] = rows[:, lo : lo + LANE]
        for d in X_ORDER:
            px = rot(x, d, NX)
            send(xs.at[r, px], xr[r].at[x], recv("x", 0, r), fid(px, z, c))
        xr[r][x] = xs[r, x]

    def p_exchange(r):
        with jax.named_scope("p_spread_wait"):
            wait_bytes(all_but_one(xr[r]), recv("x", 0, r))

        def slots(pz, dst):
            for s in range(SLOTS):
                l = tbl[0, fid(s // NC, pz, s % NC)]
                dst[s] = xr[r][l // COLBLK, lax.rem(l, COLBLK)]

        for d in Z_ORDER:
            pz = rot(z, d, NZ)
            slots(pz, zs.at[r, pz])
            send(zs.at[r, pz], zr[r].at[z], recv("z", 0, r), fid(x, pz, c))
        slots(z, zr[r].at[z])

    def p_gather(r):
        with jax.named_scope("p_exchange_wait"):
            wait_bytes(all_but_one(zr[r]), recv("z", 0, r))
        for s in range(SLOTS):
            h = tbl[1, fid(s // NC, z, s % NC)]
            for i in range(HALF):
                gs[r, s, i] = zr[r][h * HALF + i, s]
        for dx, dc in near:
            px, pc = rot(x, dx, NX), rot(c, dc, NC)
            send(
                gs.at[r, px * NC + pc],
                gr.at[r, x, c],
                recv("g", 0, r),
                fid(px, z, pc),
            )
        gr[r, x, c] = gs[r, x * NC + c]

    def p_assemble(r):
        with jax.named_scope("p_gather_wait"):
            wait_bytes(all_but_one(gs.at[r]), recv("g", 0, r))
        for xx in range(NX):
            for cc in range(NC):
                for i in range(HALF):
                    blk[0, i * NC + cc, r * RC : (r + 1) * RC, xx * LANE : (xx + 1) * LANE] = gr[
                        r, xx, cc, i
                    ]

    mate = fid(x, rot(z, HALF, NZ), c)

    def f_swap(a, src):
        send(src, fx.at[a], recv("f", a, 0), mate)

    def f_spread(a, mine):
        with jax.named_scope("f_swap_wait"):
            wait_bytes(fx.at[a], recv("f", a, 0))
        theirs = fx[a]
        for xx in range(NX):
            for j in range(COLBLK):
                lo = j * BLOCK + xx * LANE
                fs[a, xx, side_here, j] = mine[:, lo : lo + LANE]
                fs[a, xx, 1 - side_here, j] = theirs[:, lo : lo + LANE]
        for d in X_ORDER:
            px = rot(x, d, NX)
            for h in range(2):
                send(
                    fs.at[a, px, h],
                    fr[a].at[pl.ds((x * 2 + h) * COLBLK, COLBLK)],
                    recv("f", a, 1),
                    fid(px, z, c),
                )
        for h in range(2):
            fr[a][pl.ds((x * 2 + h) * COLBLK, COLBLK)] = fs[a, x, h]

    def f_exchange(a):
        with jax.named_scope("f_spread_wait"):
            wait_bytes(some(fr[a], 2 * COLBLK * (NX - 1)), recv("f", a, 1))

        def slots(pz, dst):
            for s in range(SLOTS):
                dst[s] = fr[a][tbl[3, fid(s // NC, pz, s % NC)]]

        for d in Z_ORDER:
            pz = rot(z, d, NZ)
            slots(pz, fzs.at[a, pz])
            send(
                fzs.at[a, pz],
                fz.at[a, z],
                recv("f", a, 2),
                fid(x, pz, c),
                under=3 if a else 0,
            )
        slots(z, fz.at[a, z])

    def f_gather(a):
        with jax.named_scope("f_exchange_wait"):
            wait_bytes(all_but_one(fz.at[a]), recv("f", a, 2))
        for dx, dc in near:
            px, pc = rot(x, dx, NX), rot(c, dc, NC)
            send(fz.at[a, :, px * NC + pc], fg.at[a, x, c], recv("f", a, 3), fid(px, z, pc))
        for i in range(NZ):
            fg[a, x, c, i] = fz[a, i, x * NC + c]

    def f_assemble(a, first):
        with jax.named_scope("f_gather_wait"):
            wait_bytes(some(fz.at[a], NZ - 1), recv("f", a, 3))
        for xx in range(NX):
            for cc in range(NC):
                for i in range(NZ):
                    lo = (first + i // HALF) * RC
                    blk[a, i % HALF * NC + cc, lo : lo + RC, xx * LANE : (xx + 1) * LANE] = fg[
                        a, xx, cc, i
                    ]

    def m_spread(r):
        for d in X_ORDER:
            send(ms.at[r], mx[r].at[x], recv("x", 1, FOLD + r), fid(rot(x, d, NX), z, c))
        mx[r][x] = ms[r]

    def m_exchange(r):
        with jax.named_scope("m_spread_wait"):
            wait_bytes(all_but_one(mx[r]), recv("x", 1, FOLD + r))

        def slot(pz, pc, dst):
            l = tbl[0, fid(x, pz, pc)]
            dst[...] = mx[r][l // COLBLK, lax.rem(l, COLBLK)]

        for d in Z_ORDER + (0,):
            pz = rot(z, d, NZ)
            for dc in range(NC):
                pc = rot(c, dc, NC)
                if d or dc:
                    slot(pz, pc, mzs.at[r, pz * NC + pc])
                    send(
                        mzs.at[r, pz * NC + pc],
                        mz[r].at[z * NC + c],
                        recv("z", 1, FOLD + r),
                        fid(x, pz, pc),
                    )
        slot(z, c, mz[r].at[z * NC + c])


    def m_assemble(r):
        with jax.named_scope("m_exchange_wait"):
            wait_bytes(all_but_one(mz[r]), recv("z", 1, FOLD + r))
        h = tbl[1, f]
        for i in range(HALF):
            for cc in range(NC):
                lo = (FOLD + r) * RC
                blk[1, i * NC + cc, lo : lo + RC, :] = mz[r][(h * HALF + i) * NC + cc]

    def d_exchange(r, upd):
        for i in range(HALF):
            for cc in range(NC):
                lo = (i * NC + cc) * RC
                uds[r, i, cc] = upd[lo : lo + RC, :]
        for d in Z_ORDER + (0,):
            pz = rot(z, d, NZ)
            for dc in range(NC):
                pc = rot(c, dc, NC)
                if d or dc:
                    send(
                        uds.at[r, lax.rem(pz, HALF), pc],
                        udz[r].at[z * NC + c],
                        recv("z", 2, r),
                        fid(x, pz, pc),
                    )
        udz[r][z * NC + c] = uds[r, lax.rem(z, HALF), c]

    def d_gather(r):
        with jax.named_scope("d_exchange_wait"):
            wait_bytes(all_but_one(udz[r]), recv("z", 2, r))
        for d in X_ORDER + (0,):
            px = rot(x, d, NX)
            for j in range(COLBLK):
                t = tgt_s[0, (px * 2 + side_here) * COLBLK + j]
                part = udz[r][lax.rem(t, NZ * NC)]
                if d:
                    udp[r, px, j] = part
                else:
                    udx[r][x, j] = part
            if d:
                send(udp.at[r, px], udx[r].at[x], recv("x", 2, r), fid(px, z, c))

    def d_finish(r):
        with jax.named_scope("d_gather_wait"):
            wait_bytes(all_but_one(udx[r]), recv("x", 2, r))
        for j in range(COLBLK):
            t = tgt_s[0, (x * 2 + side_here) * COLBLK + j]
            out_v[r * RC : (r + 1) * RC, j * BLOCK : (j + 1) * BLOCK] = udx[r][t // (NZ * NC), j]

    me = x * NC + c

    def u_spread(r, upd):
        for xx in range(NX):
            for cc in range(NC):
                for i in range(HALF):
                    lo = (i * NC + cc) * RC
                    ub[r, xx, cc, i] = upd[lo : lo + RC, xx * LANE : (xx + 1) * LANE]
        for dx, dc in near:
            px, pc = rot(x, dx, NX), rot(c, dc, NC)
            send(ub.at[r, px, pc], ug.at[r, me], recv("g", 2, r), fid(px, z, pc))
        ug[r, me] = ub[r, x, c]

    def u_exchange(r):
        with jax.named_scope("u_spread_wait"):
            wait_bytes(all_but_one(ug.at[r]), recv("g", 2, r))
        for d in Z_ORDER:
            pz = rot(z, d, NZ)
            send(
                ug.at[r, :, lax.rem(pz, HALF)],
                uz[r].at[z],
                recv("z", 2, r),
                fid(x, pz, c),
            )
        for s in range(SLOTS):
            uz[r][z, s] = ug[r, s, lax.rem(z, HALF)]

    def u_gather(r):
        with jax.named_scope("u_exchange_wait"):
            wait_bytes(all_but_one(uz[r]), recv("z", 2, r))
        for d in X_ORDER + (0,):
            px = rot(x, d, NX)
            for j in range(COLBLK):
                t = tgt_s[0, (px * 2 + side_here) * COLBLK + j]
                slot = (t // (NC * NZ)) * NC + lax.rem(t, NC)
                part = uz[r][lax.rem(t // NC, NZ), slot]
                if d:
                    us[r, px, j] = part
                else:
                    uf[r, x, j] = part
            if d:
                send(us.at[r, px], uf.at[r, x], recv("x", 2, r), fid(px, z, c))

    def u_finish(r):
        with jax.named_scope("u_gather_wait"):
            wait_bytes(all_but_one(uf.at[r]), recv("x", 2, r))
        for xx in range(NX):
            for j in range(COLBLK):
                lo = j * BLOCK + xx * LANE
                out_v[r * RC : (r + 1) * RC, lo : lo + LANE] = uf[r, xx, j]

    def uf_spread(upds):
        for h in range(2):
            for xx in range(NX):
                for cc in range(NC):
                    for i in range(HALF):
                        lo = (i * NC + cc) * RC
                        fub[xx, cc, h * HALF + i] = upds[h][
                            lo : lo + RC, xx * LANE : (xx + 1) * LANE
                        ]
        for dx, dc in near:
            px, pc = rot(x, dx, NX), rot(c, dc, NC)
            send(fub.at[px, pc], fug.at[me], recv("f", 4), fid(px, z, pc))
        fug[me] = fub[x, c]

    def uf_exchange():
        with jax.named_scope("uf_spread_wait"):
            wait_bytes(all_but_one(fug), recv("f", 4))
        for d in Z_ORDER:
            pz = rot(z, d, NZ)
            send(fug.at[:, pz], fuz.at[z], recv("f", 5), fid(x, pz, c), under=2)
        for s in range(SLOTS):
            fuz[z, s] = fug[s, z]

    def uf_gather():
        with jax.named_scope("uf_exchange_wait"):
            wait_bytes(all_but_one(fuz), recv("f", 5))
        for i, h in enumerate((1 - side_here, side_here)):
            for d in X_ORDER + (0,):
                px = rot(x, d, NX)
                for j in range(COLBLK):
                    t = tgt_s[0, (px * 2 + h) * COLBLK + j]
                    slot = (t // (NC * NZ)) * NC + lax.rem(t, NC)
                    part = fuz[lax.rem(t // NC, NZ), slot]
                    if d:
                        fus[h, px, j] = part
                    else:
                        fuf[h, x, j] = part
                if d:
                    send(
                        fus.at[h, px],
                        fuf.at[h, x],
                        recv("s", d) if i == 0 else recv("f", 8),
                        fid(px, z, c),
                    )

    def uf_swap():
        for d in (0,) + X_ORDER[1:] + X_ORDER[:1]:
            xx = rot(x, NX - d, NX)
            piece = fuf.at[1 - side_here, xx]
            if d:
                with jax.named_scope("uf_gather_wait"):
                    wait_bytes(piece, recv("s", d))
            send(piece, fsr.at[xx], recv("f", 7), mate)

    def uf_keep():
        wait_bytes(some(fuf.at[0], NX - 1), recv("f", 8))
        rows = pl.ds(pl.multiple_of((FOLD + side_here) * RC, RC), RC)
        for xx in range(NX):
            for j in range(COLBLK):
                lo = j * BLOCK + xx * LANE
                out_v[rows, lo : lo + LANE] = fuf[side_here, xx, j]

    def uf_finish():
        with jax.named_scope("uf_swap_wait"):
            wait_bytes(fsr, recv("f", 7))
        rows = pl.ds(pl.multiple_of((FOLD + 1 - side_here) * RC, RC), RC)
        for xx in range(NX):
            for j in range(COLBLK):
                lo = j * BLOCK + xx * LANE
                out_v[rows, lo : lo + LANE] = fsr[xx, j]

    for d in Z_ORDER:
        send(norm_s.at[0], norm_z.at[z], recv("n", 0), fid(x, rot(z, d, NZ), c))
    p_spread(0, g_v[:RC, :])
    f_swap(0, g_v.at[pl.ds(pl.multiple_of((FOLD + 1 - side_here) * RC, RC), RC), :])
    p_spread(1, g_v[RC : 2 * RC, :])

    for load in tgt_loads:
        load.wait()
    n_blocks = tgt_v.shape[1]
    sub = lax.broadcasted_iota(jnp.int32, (n_blocks, 128), 0)
    lane = lax.broadcasted_iota(jnp.int32, (n_blocks, 128), 1)
    sub_sq = lax.broadcasted_iota(jnp.int32, (n_blocks, n_blocks), 0)
    lane_sq = lax.broadcasted_iota(jnp.int32, (n_blocks, n_blocks), 1)
    diag = jnp.where(sub_sq == lane_sq, jnp.broadcast_to(tgt_v[...], sub_sq.shape), 0)
    named = jnp.sum(diag, axis=1, keepdims=True) == lane
    band = sub // COLBLK
    side = lax.rem(band, 2)
    local = jnp.where(side == side_here, sub - (band - band // 2) * COLBLK, 0)
    for i, code in enumerate((local, side, jnp.ones_like(sub), sub)):
        tbl_v[i : i + 1, :] = jnp.max(jnp.where(named, code, 0), axis=0, keepdims=True)
    tbl_copy = pltpu.make_async_copy(tbl_v, tbl, in_sem.at[5])
    tbl_copy.start()

    with jax.named_scope("norm_z_wait"):
        wait_bytes(all_but_one(norm_z), recv("n", 0))
    acc = jnp.sum(norm_z[...], axis=0)
    norm_s[1] = acc
    norm_y[q] = acc
    for d in range(1, n_mp):
        send(norm_s.at[1], norm_y.at[q], recv("n", 1), f, rot(q, d, n_mp))
    tbl_copy.wait()
    p_exchange(0)
    with jax.named_scope("norm_y_wait"):
        wait_bytes(all_but_one(norm_y), recv("n", 1))
    acc = jnp.sum(norm_y[...], axis=0)
    norm_s[2] = acc
    norm_x[me] = acc
    for dx, dc in near:
        send(
            norm_s.at[2],
            norm_x.at[me],
            recv("n", 2),
            fid(rot(x, dx, NX), z, rot(c, dc, NC)),
        )
    p_exchange(1)
    f_spread(0, g_v[pl.ds(pl.multiple_of((FOLD + side_here) * RC, RC), RC), :])
    with jax.named_scope("norm_x_wait"):
        wait_bytes(all_but_one(norm_x), recv("n", 2))
    acc = jnp.sum(norm_x[...], axis=0)
    norm_sum = jnp.sum(jnp.sum(acc, axis=0, keepdims=True), axis=1, keepdims=True)
    clip = jnp.minimum(1.0, CLIP_RMS * (float(n_entries) ** 0.5) / jnp.sqrt(norm_sum))

    loads[1].wait()
    for r in range(CHUNKS):
        rows = slice(r * RC, (r + 1) * RC)
        nxt = FIRST_DECAY * f_v[rows, :] + ((1.0 - FIRST_DECAY) * clip) * g_v[rows, :].astype(F32)
        f_v[rows, :] = nxt
        low = nxt.astype(BF16)
        if r < FOLD:
            mf[r] = low
            if r == FOLD - 1:
                f_swap(1, mf.at[1 - side_here])
        else:
            for j in range(COLBLK):
                ms[r - FOLD, j] = low[:, j * BLOCK : (j + 1) * BLOCK]
            m_spread(r - FOLD)
    wait_units(1024, in_sem.at[2])
    qlt_v[...] = ql_v[...].reshape(BLOCK, BLOCK).T
    qrt_v[...] = qr_v[...].T
    f_exchange(0)
    p_gather(0)
    m_exchange(0)
    f_spread(1, mf[side_here])
    p_gather(1)
    f_exchange(1)
    f_gather(0)

    for r in range(FOLD):
        p_assemble(r)
    f_assemble(0, FOLD)
    with jax.named_scope("owner_gradient"):
        live = tbl[2, f] > 0
        block = blk[0].reshape(BLOCK, BLOCK)
        half = mm(qlt_v[...], block).astype(BF16)
        rotated = clip * mm(half, qr_v[...])
        second = SECOND_DECAY * sm_v[...] + SECOND_RATE * rotated * rotated
        den_v[...] = jnp.sqrt(second) + EPSILON
        sm_v[...] = jnp.where(live, second, sm_v[...])
        scale = GRAM_RATE * clip * clip / BLOCK
        block_t = block.T
        lg_v[...] = jnp.where(live, GRAM_DECAY * lg_v[...] + scale * mm(block, block_t), lg_v[...])
        rg_v[...] = jnp.where(live, GRAM_DECAY * rg_v[...] + scale * mm(block_t, block), rg_v[...])

    wait_units(sent[3], send_sem.at[3])
    m_exchange(1)

    f_gather(1)
    f_assemble(1, 0)
    for r in range(CHUNKS - FOLD):
        m_assemble(r)
    with jax.named_scope("owner_moment"):
        mhalf = mm(qlt_v[...], blk[1].reshape(BLOCK, BLOCK)).astype(BF16)
        normed = (mm(mhalf, qr_v[...]) / den_v[...]).astype(BF16)

    def update(r):
        rows = ql_v[:, r * RC : (r + 1) * RC, :].reshape(HALF * NC * RC, BLOCK)
        return mm(mm(rows, normed).astype(BF16), qrt_v[...]).astype(BF16)

    group[0] = 1
    d_exchange(0, update(0))
    uf_spread([update(FOLD), update(FOLD + 1)])
    upd = update(1)

    wait_units(sent[0], send_sem.at[0])

    uf_exchange()
    u_spread(1, upd)
    d_gather(0)
    with jax.named_scope("uf_sent_wait"):
        wait_units(sent[2], send_sem.at[2])
    u_exchange(1)
    uf_gather()
    uf_swap()
    u_gather(1)
    uf_keep()
    d_finish(0)
    u_finish(1)
    uf_finish()
    wait_units(sent[1], send_sem.at[1])


def write_out(*refs):
    n = (len(refs) - 1) // 2
    copies = [
        pltpu.make_async_copy(refs[i], refs[n + i], refs[-1].at[i]) for i in range(n)
    ]
    for copy in copies:
        copy.start()
    for copy in copies:
        copy.wait()


def shards(
    gradient,
    first_moment,
    left_gram,
    right_gram,
    left_basis,
    right_basis,
    second_moment,
    block_target,
):
    rows, cols = gradient.shape
    n_fsdp = lax.axis_size("fsdp")
    n_mp = lax.axis_size("mp")
    n_blocks = block_target.shape[1]
    any_spec = pl.BlockSpec(memory_space=pl.ANY)
    vmem_spec = pl.BlockSpec(memory_space=pltpu.VMEM)
    vm = pltpu.VMEM
    dma = pltpu.SemaphoreType.DMA
    mat = (BLOCK, BLOCK)
    piece = (RC, LANE)
    strip = (RC, BLOCK)

    def per_chunk(n, *shape):
        return [vm(shape, BF16) for _ in range(n)]

    shapes = [((rows, cols), BF16), ((rows, cols), F32)] + [(mat, F32)] * 3
    held = pl.pallas_call(
        functools.partial(kernel, rows * cols * n_fsdp * n_mp),
        out_shape=tuple(vm(s, d) for s, d in shapes),
        in_specs=[any_spec] * 8,
        out_specs=(vmem_spec,) * 5,
        scratch_shapes=[
            vm((rows, cols), BF16),
            vm((HALF * NC, ROWS, BLOCK), BF16),
            vm(mat, BF16),
            vm(mat, BF16),
            vm(mat, BF16),
            vm(mat, F32),
            vm((3, 8, 128), F32),
            vm((n_mp, 8, 128), F32),
            vm((SLOTS, 8, 128), F32),
            vm((NZ, 8, 128), F32),
            vm((FOLD, NX, COLBLK) + piece, BF16),
            per_chunk(FOLD, NX, COLBLK, *piece),
            vm((FOLD, NZ, SLOTS) + piece, BF16),
            per_chunk(FOLD, NZ, SLOTS, *piece),
            vm((FOLD, SLOTS, HALF) + piece, BF16),
            vm((FOLD, NX, NC, HALF) + piece, BF16),
            vm((2, RC, cols), BF16),
            vm((2, RC, cols), BF16),
            vm((2, NX, 2, COLBLK) + piece, BF16),
            per_chunk(2, 2 * LOCAL, *piece),
            vm((2, NZ, SLOTS) + piece, BF16),
            vm((2, NZ, SLOTS) + piece, BF16),
            vm((2, NX, NC, NZ) + piece, BF16),
            vm((2, HALF * NC, ROWS, BLOCK), BF16),
            vm((CHUNKS - FOLD, COLBLK) + strip, BF16),
            per_chunk(CHUNKS - FOLD, NX, COLBLK, *strip),
            vm((CHUNKS - FOLD, NZ * NC) + strip, BF16),
            per_chunk(CHUNKS - FOLD, NZ * NC, *strip),
            vm((DIRECT, HALF, NC) + strip, BF16),
            per_chunk(DIRECT, NZ * NC, *strip),
            vm((DIRECT, NX, COLBLK) + strip, BF16),
            per_chunk(DIRECT, NX, COLBLK, *strip),
            vm((NX, NC, NZ) + piece, BF16),
            vm((SLOTS, NZ) + piece, BF16),
            vm((NZ, SLOTS) + piece, BF16),
            vm((2, NX, COLBLK) + piece, BF16),
            vm((2, NX, COLBLK) + piece, BF16),
            vm((NX, COLBLK) + piece, BF16),
            vm((CHUNKS, NX, NC, HALF) + piece, BF16),
            vm((CHUNKS, SLOTS, HALF) + piece, BF16),
            per_chunk(CHUNKS, NZ, SLOTS, *piece),
            vm((CHUNKS, NX, COLBLK) + piece, BF16),
            vm((CHUNKS, NX, COLBLK) + piece, BF16),
            pltpu.SMEM((1, n_blocks), jnp.int32),
            vm((1, n_blocks), jnp.int32),
            vm((8, 128), jnp.int32),
            pltpu.SMEM((8, 128), jnp.int32),
            vm((1024, RC, LANE), BF16),
            dma((6,)),
            dma((4,)),
            dma((len(RECV),)),
        ],
        compiler_params=pltpu.CompilerParams(
            collective_id=0, has_side_effects=True, vmem_limit_bytes=59 * 2**20
        ),
        cost_estimate=pl.CostEstimate(
            flops=16 * BLOCK**3, bytes_accessed=12 * 2**20, transcendentals=BLOCK**2
        ),
    )(
        block_target,
        gradient,
        first_moment,
        left_gram[0, 0],
        right_gram[0, 0],
        left_basis[0, 0].reshape(HALF * NC, ROWS, BLOCK),
        right_basis[0, 0],
        second_moment[0, 0],
    )
    out = pl.pallas_call(
        write_out,
        out_shape=tuple(jax.ShapeDtypeStruct(s, d) for s, d in shapes),
        in_specs=[vmem_spec] * 5,
        out_specs=(any_spec,) * 5,
        scratch_shapes=[dma((5,))],
        compiler_params=pltpu.CompilerParams(vmem_limit_bytes=2**20),
    )(*held)
    return (out[0], out[1]) + tuple(o[None, None] for o in out[2:])


def solution(mesh):
    return jax.shard_map(
        shards,
        mesh=mesh,
        in_specs=(
            P("fsdp", "mp"),
            P("fsdp", "mp"),
            P("fsdp", "mp", None, None),
            P("fsdp", "mp", None, None),
            P("fsdp", "mp", None, None),
            P("fsdp", "mp", None, None),
            P("fsdp", "mp", None, None),
            P("mp", None),
        ),
        out_specs=(
            P("fsdp", "mp"),
            P("fsdp", "mp"),
            P("fsdp", "mp", None, None),
            P("fsdp", "mp", None, None),
            P("fsdp", "mp", None, None),
        ),
        check_vma=False,
    )
```

```python
import functools
import math

import jax
import jax.numpy as jnp
from jax import lax
from jax.experimental import pallas as pl
from jax.experimental.pallas import tpu as pltpu
from jax.sharding import PartitionSpec as P

CLIP_RMS = 0.5
FIRST_DECAY = 0.9
GRAM_DECAY = 0.95
GRAM_RATE = 0.05
SECOND_DECAY = 0.95
SECOND_RATE = 0.05
EPSILON = 1e-08

MESH = pl.DeviceIdType.MESH
NX, NZ, NC = 4, 8, 2
HALF = NZ // 2
COLBLK = 7
SLOTS = NX * NC
LOCAL = NX * COLBLK
ROWS = 64
BLOCK = 512
LANE = BLOCK // NX
CHUNKS = 4
FOLD = 2
DIRECT = 1
RC = ROWS // CHUNKS
Z_ORDER = (4, 5, 3, 6, 2, 7, 1)
X_ORDER = (2, 1, 3)

UNIT = RC * LANE * 2
PLAIN = [(0, r) for r in range(FOLD)]
LATER = [(1, r) for r in range(FOLD, CHUNKS)] + [(2, 0), (2, 1)]
RECV = [(k,) + ar for k in "xz" for ar in PLAIN + LATER]
RECV += [("g",) + ar for ar in PLAIN + [(2, 1)]]
RECV += [("f", a, i) for a in range(2) for i in range(4)] + [("f", i) for i in (4, 5, 7, 8)] + [("s", d) for d in X_ORDER] + [("n", i) for i in range(3)]

BF16, F32 = jnp.bfloat16, jnp.float32


def mm(a, b):
    return jnp.dot(a, b, preferred_element_type=F32)


def kernel(
    n_entries,
    tgt_hbm,
    grad_hbm,
    first_hbm,
    lg_hbm,
    rg_hbm,
    ql_hbm,
    qr_hbm,
    sm_hbm,
    out_v,
    f_v,
    lg_v,
    rg_v,
    sm_v,
    g_v,
    ql_v,
    qr_v,
    qlt_v,
    qrt_v,
    den_v,
    norm_s,
    norm_y,
    norm_x,
    norm_z,
    xs,
    xr,
    zs,
    zr,
    gs,
    gr,
    mf,
    fx,
    fs,
    fr,
    fzs,
    fz,
    fg,
    blk,
    ms,
    mx,
    mzs,
    mz,
    uds,
    udz,
    udp,
    udx,
    fub,
    fug,
    fuz,
    fus,
    fuf,
    fsr,
    ub,
    ug,
    uz,
    us,
    uf,
    tgt_s,
    tgt_v,
    tbl_v,
    tbl,
    units,
    in_sem,
    send_sem,
    recv_sem,
):
    f = lax.axis_index("fsdp")
    q = lax.axis_index("mp")
    c = lax.rem(f, NC)
    z = lax.rem(f // NC, NZ)
    x = f // (NC * NZ)
    side_here = z // HALF
    n_mp = lax.axis_size("mp")

    def fid(xx, zz, cc):
        return (xx * NZ + zz) * NC + cc

    def rot(v, d, n):
        return lax.rem(v + d, n)

    near = [(dx, dc) for dx in X_ORDER + (0,) for dc in range(NC) if dx or dc]
    barrier = pltpu.get_barrier_semaphore()
    peers = [(fid(x, rot(z, d, NZ), rot(c, dc, NC)), q) for d in Z_ORDER for dc in range(NC)]
    peers += [(fid(rot(x, dx, NX), z, rot(c, dc, NC)), q) for dx, dc in near]
    peers += [(f, rot(q, d, n_mp)) for d in range(1, n_mp)]
    for peer in peers:
        pl.semaphore_signal(barrier, inc=1, device_id=peer, device_id_type=MESH)

    tgt_loads = [
        pltpu.make_async_copy(tgt_hbm, tgt_s, in_sem.at[3]),
        pltpu.make_async_copy(tgt_hbm, tgt_v, in_sem.at[4]),
    ]
    loads = [
        pltpu.make_async_copy(src, dst, in_sem.at[min(i, 2)])
        for i, (src, dst) in enumerate(
            (
                (grad_hbm, g_v),
                (first_hbm, f_v),
                (ql_hbm, ql_v),
                (qr_hbm, qr_v),
                (sm_hbm, sm_v),
                (lg_hbm, lg_v),
                (rg_hbm, rg_v),
            )
        )
    ]
    for load in loads[:1] + tgt_loads + loads[1:]:
        load.start()

    loads[0].wait()
    wide = g_v[...].astype(F32)
    cols = jnp.sum((wide * wide).reshape(ROWS // 8, 8, wide.shape[1]), axis=0)
    acc = cols[:, :128]
    for i in range(1, cols.shape[1] // 128):
        acc = acc + cols[:, i * 128 : (i + 1) * 128]
    norm_s[0] = acc
    norm_z[z] = acc

    with jax.named_scope("barrier"):
        pl.semaphore_wait(barrier, len(peers))

    sent = [0, 0, 0, 0]
    group = [0]

    def send(src, dst, rsem, pf, pq=q, under=None):
        under = group[0] if under is None else under
        sent[under] += math.prod(src.shape) * src.dtype.itemsize // UNIT
        pltpu.make_async_remote_copy(
            src_ref=src,
            dst_ref=dst,
            send_sem=send_sem.at[under],
            recv_sem=rsem,
            device_id=(pf, pq),
            device_id_type=MESH,
        ).start()

    def recv(*key):
        return recv_sem.at[RECV.index(key)]

    def wait_units(n, sem):
        wait_bytes(units.at[pl.ds(0, n)], sem)

    def wait_bytes(ref, sem):
        pltpu.make_async_copy(ref, ref, sem).wait()

    def some(ref, n):
        return ref.at[pl.ds(0, n)]

    def all_but_one(ref):
        return some(ref, ref.shape[0] - 1)

    def p_spread(r, rows):
        for xx in range(NX):
            for j in range(COLBLK):
                lo = j * BLOCK + xx * LANE
                xs[r, xx, j] = rows[:, lo : lo + LANE]
        for d in X_ORDER:
            px = rot(x, d, NX)
            send(xs.at[r, px], xr[r].at[x], recv("x", 0, r), fid(px, z, c))
        xr[r][x] = xs[r, x]

    def p_exchange(r):
        with jax.named_scope("p_spread_wait"):
            wait_bytes(all_but_one(xr[r]), recv("x", 0, r))

        def slots(pz, dst):
            for s in range(SLOTS):
                l = tbl[0, fid(s // NC, pz, s % NC)]
                dst[s] = xr[r][l // COLBLK, lax.rem(l, COLBLK)]

        for d in Z_ORDER:
            pz = rot(z, d, NZ)
            slots(pz, zs.at[r, pz])
            send(zs.at[r, pz], zr[r].at[z], recv("z", 0, r), fid(x, pz, c))
        slots(z, zr[r].at[z])

    def p_gather(r):
        with jax.named_scope("p_exchange_wait"):
            wait_bytes(all_but_one(zr[r]), recv("z", 0, r))
        for s in range(SLOTS):
            h = tbl[1, fid(s // NC, z, s % NC)]
            for i in range(HALF):
                gs[r, s, i] = zr[r][h * HALF + i, s]
        for dx, dc in near:
            px, pc = rot(x, dx, NX), rot(c, dc, NC)
            send(
                gs.at[r, px * NC + pc],
                gr.at[r, x, c],
                recv("g", 0, r),
                fid(px, z, pc),
            )
        gr[r, x, c] = gs[r, x * NC + c]

    def p_assemble(r):
        with jax.named_scope("p_gather_wait"):
            wait_bytes(all_but_one(gs.at[r]), recv("g", 0, r))
        for xx in range(NX):
            for cc in range(NC):
                for i in range(HALF):
                    blk[0, i * NC + cc, r * RC : (r + 1) * RC, xx * LANE : (xx + 1) * LANE] = gr[
                        r, xx, cc, i
                    ]

    mate = fid(x, rot(z, HALF, NZ), c)

    def f_swap(a, src):
        send(src, fx.at[a], recv("f", a, 0), mate)

    def f_spread(a, mine):
        with jax.named_scope("f_swap_wait"):
            wait_bytes(fx.at[a], recv("f", a, 0))
        theirs = fx[a]
        for xx in range(NX):
            for j in range(COLBLK):
                lo = j * BLOCK + xx * LANE
                fs[a, xx, side_here, j] = mine[:, lo : lo + LANE]
                fs[a, xx, 1 - side_here, j] = theirs[:, lo : lo + LANE]
        for d in X_ORDER:
            px = rot(x, d, NX)
            for h in range(2):
                send(
                    fs.at[a, px, h],
                    fr[a].at[pl.ds((x * 2 + h) * COLBLK, COLBLK)],
                    recv("f", a, 1),
                    fid(px, z, c),
                )
        for h in range(2):
            fr[a][pl.ds((x * 2 + h) * COLBLK, COLBLK)] = fs[a, x, h]

    def f_exchange(a):
        with jax.named_scope("f_spread_wait"):
            wait_bytes(some(fr[a], 2 * COLBLK * (NX - 1)), recv("f", a, 1))

        def slots(pz, dst):
            for s in range(SLOTS):
                dst[s] = fr[a][tbl[3, fid(s // NC, pz, s % NC)]]

        for d in Z_ORDER:
            pz = rot(z, d, NZ)
            slots(pz, fzs.at[a, pz])
            send(
                fzs.at[a, pz],
                fz.at[a, z],
                recv("f", a, 2),
                fid(x, pz, c),
                under=3 if a else 0,
            )
        slots(z, fz.at[a, z])

    def f_gather(a):
        with jax.named_scope("f_exchange_wait"):
            wait_bytes(all_but_one(fz.at[a]), recv("f", a, 2))
        for dx, dc in near:
            px, pc = rot(x, dx, NX), rot(c, dc, NC)
            send(fz.at[a, :, px * NC + pc], fg.at[a, x, c], recv("f", a, 3), fid(px, z, pc))
        for i in range(NZ):
            fg[a, x, c, i] = fz[a, i, x * NC + c]

    def f_assemble(a, first):
        with jax.named_scope("f_gather_wait"):
            wait_bytes(some(fz.at[a], NZ - 1), recv("f", a, 3))
        for xx in range(NX):
            for cc in range(NC):
                for i in range(NZ):
                    lo = (first + i // HALF) * RC
                    blk[a, i % HALF * NC + cc, lo : lo + RC, xx * LANE : (xx + 1) * LANE] = fg[
                        a, xx, cc, i
                    ]

    def m_spread(r):
        for d in X_ORDER:
            send(ms.at[r], mx[r].at[x], recv("x", 1, FOLD + r), fid(rot(x, d, NX), z, c))
        mx[r][x] = ms[r]

    def m_exchange(r):
        with jax.named_scope("m_spread_wait"):
            wait_bytes(all_but_one(mx[r]), recv("x", 1, FOLD + r))

        def slot(pz, pc, dst):
            l = tbl[0, fid(x, pz, pc)]
            dst[...] = mx[r][l // COLBLK, lax.rem(l, COLBLK)]

        for d in Z_ORDER + (0,):
            pz = rot(z, d, NZ)
            for dc in range(NC):
                pc = rot(c, dc, NC)
                if d or dc:
                    slot(pz, pc, mzs.at[r, pz * NC + pc])
                    send(
                        mzs.at[r, pz * NC + pc],
                        mz[r].at[z * NC + c],
                        recv("z", 1, FOLD + r),
                        fid(x, pz, pc),
                    )
        slot(z, c, mz[r].at[z * NC + c])


    def m_assemble(r):
        with jax.named_scope("m_exchange_wait"):
            wait_bytes(all_but_one(mz[r]), recv("z", 1, FOLD + r))
        h = tbl[1, f]
        for i in range(HALF):
            for cc in range(NC):
                lo = (FOLD + r) * RC
                blk[1, i * NC + cc, lo : lo + RC, :] = mz[r][(h * HALF + i) * NC + cc]

    def d_exchange(r, upd):
        for i in range(HALF):
            for cc in range(NC):
                lo = (i * NC + cc) * RC
                uds[r, i, cc] = upd[lo : lo + RC, :]
        for d in Z_ORDER + (0,):
            pz = rot(z, d, NZ)
            for dc in range(NC):
                pc = rot(c, dc, NC)
                if d or dc:
                    send(
                        uds.at[r, lax.rem(pz, HALF), pc],
                        udz[r].at[z * NC + c],
                        recv("z", 2, r),
                        fid(x, pz, pc),
                    )
        udz[r][z * NC + c] = uds[r, lax.rem(z, HALF), c]

    def d_gather(r):
        with jax.named_scope("d_exchange_wait"):
            wait_bytes(all_but_one(udz[r]), recv("z", 2, r))
        for d in X_ORDER + (0,):
            px = rot(x, d, NX)
            for j in range(COLBLK):
                t = tgt_s[0, (px * 2 + side_here) * COLBLK + j]
                part = udz[r][lax.rem(t, NZ * NC)]
                if d:
                    udp[r, px, j] = part
                else:
                    udx[r][x, j] = part
            if d:
                send(udp.at[r, px], udx[r].at[x], recv("x", 2, r), fid(px, z, c))

    def d_finish(r):
        with jax.named_scope("d_gather_wait"):
            wait_bytes(all_but_one(udx[r]), recv("x", 2, r))
        for j in range(COLBLK):
            t = tgt_s[0, (x * 2 + side_here) * COLBLK + j]
            out_v[r * RC : (r + 1) * RC, j * BLOCK : (j + 1) * BLOCK] = udx[r][t // (NZ * NC), j]

    me = x * NC + c

    def u_spread(r, upd):
        for xx in range(NX):
            for cc in range(NC):
                for i in range(HALF):
                    lo = (i * NC + cc) * RC
                    ub[r, xx, cc, i] = upd[lo : lo + RC, xx * LANE : (xx + 1) * LANE]
        for dx, dc in near:
            px, pc = rot(x, dx, NX), rot(c, dc, NC)
            send(ub.at[r, px, pc], ug.at[r, me], recv("g", 2, r), fid(px, z, pc))
        ug[r, me] = ub[r, x, c]

    def u_exchange(r):
        with jax.named_scope("u_spread_wait"):
            wait_bytes(all_but_one(ug.at[r]), recv("g", 2, r))
        for d in Z_ORDER:
            pz = rot(z, d, NZ)
            send(
                ug.at[r, :, lax.rem(pz, HALF)],
                uz[r].at[z],
                recv("z", 2, r),
                fid(x, pz, c),
            )
        for s in range(SLOTS):
            uz[r][z, s] = ug[r, s, lax.rem(z, HALF)]

    def u_gather(r):
        with jax.named_scope("u_exchange_wait"):
            wait_bytes(all_but_one(uz[r]), recv("z", 2, r))
        for d in X_ORDER + (0,):
            px = rot(x, d, NX)
            for j in range(COLBLK):
                t = tgt_s[0, (px * 2 + side_here) * COLBLK + j]
                slot = (t // (NC * NZ)) * NC + lax.rem(t, NC)
                part = uz[r][lax.rem(t // NC, NZ), slot]
                if d:
                    us[r, px, j] = part
                else:
                    uf[r, x, j] = part
            if d:
                send(us.at[r, px], uf.at[r, x], recv("x", 2, r), fid(px, z, c))

    def u_finish(r):
        with jax.named_scope("u_gather_wait"):
            wait_bytes(all_but_one(uf.at[r]), recv("x", 2, r))
        for xx in range(NX):
            for j in range(COLBLK):
                lo = j * BLOCK + xx * LANE
                out_v[r * RC : (r + 1) * RC, lo : lo + LANE] = uf[r, xx, j]

    def uf_spread(upd):
        for h in range(2):
            for xx in range(NX):
                for cc in range(NC):
                    for i in range(HALF):
                        lo = ((i * NC + cc) * 2 + h) * RC
                        fub[xx, cc, h * HALF + i] = upd[
                            lo : lo + RC, xx * LANE : (xx + 1) * LANE
                        ]
        for dx, dc in near:
            px, pc = rot(x, dx, NX), rot(c, dc, NC)
            send(fub.at[px, pc], fug.at[me], recv("f", 4), fid(px, z, pc))
        fug[me] = fub[x, c]

    def uf_exchange():
        with jax.named_scope("uf_spread_wait"):
            wait_bytes(all_but_one(fug), recv("f", 4))
        for d in Z_ORDER:
            pz = rot(z, d, NZ)
            send(fug.at[:, pz], fuz.at[z], recv("f", 5), fid(x, pz, c), under=2)
        for s in range(SLOTS):
            fuz[z, s] = fug[s, z]

    def uf_gather():
        with jax.named_scope("uf_exchange_wait"):
            wait_bytes(all_but_one(fuz), recv("f", 5))
        for i, h in enumerate((1 - side_here, side_here)):
            for d in X_ORDER + (0,):
                px = rot(x, d, NX)
                for j in range(COLBLK):
                    t = tgt_s[0, (px * 2 + h) * COLBLK + j]
                    slot = (t // (NC * NZ)) * NC + lax.rem(t, NC)
                    part = fuz[lax.rem(t // NC, NZ), slot]
                    if d:
                        fus[h, px, j] = part
                    else:
                        fuf[h, x, j] = part
                if d:
                    send(
                        fus.at[h, px],
                        fuf.at[h, x],
                        recv("s", d) if i == 0 else recv("f", 8),
                        fid(px, z, c),
                    )

    def uf_swap():
        for d in (0,) + X_ORDER[1:] + X_ORDER[:1]:
            xx = rot(x, NX - d, NX)
            piece = fuf.at[1 - side_here, xx]
            if d:
                with jax.named_scope("uf_gather_wait"):
                    wait_bytes(piece, recv("s", d))
            send(piece, fsr.at[xx], recv("f", 7), mate)

    def uf_keep():
        wait_bytes(some(fuf.at[0], NX - 1), recv("f", 8))
        rows = pl.ds(pl.multiple_of((FOLD + side_here) * RC, RC), RC)
        for xx in range(NX):
            for j in range(COLBLK):
                lo = j * BLOCK + xx * LANE
                out_v[rows, lo : lo + LANE] = fuf[side_here, xx, j]

    def uf_finish():
        with jax.named_scope("uf_swap_wait"):
            wait_bytes(fsr, recv("f", 7))
        rows = pl.ds(pl.multiple_of((FOLD + 1 - side_here) * RC, RC), RC)
        for xx in range(NX):
            for j in range(COLBLK):
                lo = j * BLOCK + xx * LANE
                out_v[rows, lo : lo + LANE] = fsr[xx, j]

    for d in Z_ORDER:
        send(norm_s.at[0], norm_z.at[z], recv("n", 0), fid(x, rot(z, d, NZ), c))
    p_spread(0, g_v[:RC, :])
    f_swap(0, g_v.at[pl.ds(pl.multiple_of((FOLD + 1 - side_here) * RC, RC), RC), :])
    p_spread(1, g_v[RC : 2 * RC, :])

    for load in tgt_loads:
        load.wait()
    n_blocks = tgt_v.shape[1]
    sub = lax.broadcasted_iota(jnp.int32, (n_blocks, 128), 0)
    lane = lax.broadcasted_iota(jnp.int32, (n_blocks, 128), 1)
    sub_sq = lax.broadcasted_iota(jnp.int32, (n_blocks, n_blocks), 0)
    lane_sq = lax.broadcasted_iota(jnp.int32, (n_blocks, n_blocks), 1)
    diag = jnp.where(sub_sq == lane_sq, jnp.broadcast_to(tgt_v[...], sub_sq.shape), 0)
    named = jnp.sum(diag, axis=1, keepdims=True) == lane
    band = sub // COLBLK
    side = lax.rem(band, 2)
    local = jnp.where(side == side_here, sub - (band - band // 2) * COLBLK, 0)
    for i, code in enumerate((local, side, jnp.ones_like(sub), sub)):
        tbl_v[i : i + 1, :] = jnp.max(jnp.where(named, code, 0), axis=0, keepdims=True)
    tbl_copy = pltpu.make_async_copy(tbl_v, tbl, in_sem.at[5])
    tbl_copy.start()

    with jax.named_scope("norm_z_wait"):
        wait_bytes(all_but_one(norm_z), recv("n", 0))
    acc = jnp.sum(norm_z[...], axis=0)
    norm_s[1] = acc
    norm_y[q] = acc
    for d in range(1, n_mp):
        send(norm_s.at[1], norm_y.at[q], recv("n", 1), f, rot(q, d, n_mp))
    tbl_copy.wait()
    p_exchange(0)
    with jax.named_scope("norm_y_wait"):
        wait_bytes(all_but_one(norm_y), recv("n", 1))
    acc = jnp.sum(norm_y[...], axis=0)
    norm_s[2] = acc
    norm_x[me] = acc
    for dx, dc in near:
        send(
            norm_s.at[2],
            norm_x.at[me],
            recv("n", 2),
            fid(rot(x, dx, NX), z, rot(c, dc, NC)),
        )
    p_exchange(1)
    f_spread(0, g_v[pl.ds(pl.multiple_of((FOLD + side_here) * RC, RC), RC), :])
    with jax.named_scope("norm_x_wait"):
        wait_bytes(all_but_one(norm_x), recv("n", 2))
    acc = jnp.sum(norm_x[...], axis=0)
    norm_sum = jnp.sum(jnp.sum(acc, axis=0, keepdims=True), axis=1, keepdims=True)
    clip = jnp.minimum(1.0, CLIP_RMS * (float(n_entries) ** 0.5) / jnp.sqrt(norm_sum))

    loads[1].wait()
    for r in range(CHUNKS):
        rows = slice(r * RC, (r + 1) * RC)
        nxt = FIRST_DECAY * f_v[rows, :] + ((1.0 - FIRST_DECAY) * clip) * g_v[rows, :].astype(F32)
        f_v[rows, :] = nxt
        low = nxt.astype(BF16)
        if r < FOLD:
            mf[r] = low
            if r == FOLD - 1:
                f_swap(1, mf.at[1 - side_here])
        else:
            for j in range(COLBLK):
                ms[r - FOLD, j] = low[:, j * BLOCK : (j + 1) * BLOCK]
            m_spread(r - FOLD)
    wait_units(1024, in_sem.at[2])
    qlt_v[...] = ql_v[...].reshape(BLOCK, BLOCK).T
    qrt_v[...] = qr_v[...].T
    f_exchange(0)
    p_gather(0)
    m_exchange(0)
    f_spread(1, mf[side_here])
    p_gather(1)
    f_exchange(1)
    f_gather(0)

    for r in range(FOLD):
        p_assemble(r)
    f_assemble(0, FOLD)
    with jax.named_scope("owner_gradient"):
        live = tbl[2, f] > 0
        block = blk[0].reshape(BLOCK, BLOCK)
        half = mm(qlt_v[...], block).astype(BF16)
        rotated = clip * mm(half, qr_v[...])
        second = SECOND_DECAY * sm_v[...] + SECOND_RATE * rotated * rotated
        den_v[...] = jnp.sqrt(second) + EPSILON
        sm_v[...] = jnp.where(live, second, sm_v[...])
        scale = GRAM_RATE * clip * clip / BLOCK
        block_t = block.T
        lg_v[...] = jnp.where(live, GRAM_DECAY * lg_v[...] + scale * mm(block, block_t), lg_v[...])
        rg_v[...] = jnp.where(live, GRAM_DECAY * rg_v[...] + scale * mm(block_t, block), rg_v[...])

    wait_units(sent[3], send_sem.at[3])
    m_exchange(1)

    f_gather(1)
    f_assemble(1, 0)
    for r in range(CHUNKS - FOLD):
        m_assemble(r)
    with jax.named_scope("owner_moment"):
        mhalf = mm(qlt_v[...], blk[1].reshape(BLOCK, BLOCK)).astype(BF16)
        normed = (mm(mhalf, qr_v[...]) / den_v[...]).astype(BF16)

    def update(r, n=1):
        rows = ql_v[:, r * RC : (r + n) * RC, :].reshape(HALF * NC * n * RC, BLOCK)
        return mm(mm(rows, normed).astype(BF16), qrt_v[...]).astype(BF16)

    group[0] = 1
    d_exchange(0, update(0))
    uf_spread(update(FOLD, 2))
    upd = update(1)

    wait_units(sent[0], send_sem.at[0])

    uf_exchange()
    u_spread(1, upd)
    d_gather(0)
    with jax.named_scope("uf_sent_wait"):
        wait_units(sent[2], send_sem.at[2])
    u_exchange(1)
    uf_gather()
    uf_swap()
    u_gather(1)
    uf_keep()
    d_finish(0)
    u_finish(1)
    uf_finish()
    wait_units(sent[1], send_sem.at[1])


def write_out(*refs):
    n = (len(refs) - 1) // 2
    copies = [
        pltpu.make_async_copy(refs[i], refs[n + i], refs[-1].at[i]) for i in range(n)
    ]
    for copy in copies:
        copy.start()
    for copy in copies:
        copy.wait()


def shards(
    gradient,
    first_moment,
    left_gram,
    right_gram,
    left_basis,
    right_basis,
    second_moment,
    block_target,
):
    rows, cols = gradient.shape
    n_fsdp = lax.axis_size("fsdp")
    n_mp = lax.axis_size("mp")
    n_blocks = block_target.shape[1]
    any_spec = pl.BlockSpec(memory_space=pl.ANY)
    vmem_spec = pl.BlockSpec(memory_space=pltpu.VMEM)
    vm = pltpu.VMEM
    dma = pltpu.SemaphoreType.DMA
    mat = (BLOCK, BLOCK)
    piece = (RC, LANE)
    strip = (RC, BLOCK)

    def per_chunk(n, *shape):
        return [vm(shape, BF16) for _ in range(n)]

    shapes = [((rows, cols), BF16), ((rows, cols), F32)] + [(mat, F32)] * 3
    held = pl.pallas_call(
        functools.partial(kernel, rows * cols * n_fsdp * n_mp),
        out_shape=tuple(vm(s, d) for s, d in shapes),
        in_specs=[any_spec] * 8,
        out_specs=(vmem_spec,) * 5,
        scratch_shapes=[
            vm((rows, cols), BF16),
            vm((HALF * NC, ROWS, BLOCK), BF16),
            vm(mat, BF16),
            vm(mat, BF16),
            vm(mat, BF16),
            vm(mat, F32),
            vm((3, 8, 128), F32),
            vm((n_mp, 8, 128), F32),
            vm((SLOTS, 8, 128), F32),
            vm((NZ, 8, 128), F32),
            vm((FOLD, NX, COLBLK) + piece, BF16),
            per_chunk(FOLD, NX, COLBLK, *piece),
            vm((FOLD, NZ, SLOTS) + piece, BF16),
            per_chunk(FOLD, NZ, SLOTS, *piece),
            vm((FOLD, SLOTS, HALF) + piece, BF16),
            vm((FOLD, NX, NC, HALF) + piece, BF16),
            vm((2, RC, cols), BF16),
            vm((2, RC, cols), BF16),
            vm((2, NX, 2, COLBLK) + piece, BF16),
            per_chunk(2, 2 * LOCAL, *piece),
            vm((2, NZ, SLOTS) + piece, BF16),
            vm((2, NZ, SLOTS) + piece, BF16),
            vm((2, NX, NC, NZ) + piece, BF16),
            vm((2, HALF * NC, ROWS, BLOCK), BF16),
            vm((CHUNKS - FOLD, COLBLK) + strip, BF16),
            per_chunk(CHUNKS - FOLD, NX, COLBLK, *strip),
            vm((CHUNKS - FOLD, NZ * NC) + strip, BF16),
            per_chunk(CHUNKS - FOLD, NZ * NC, *strip),
            vm((DIRECT, HALF, NC) + strip, BF16),
            per_chunk(DIRECT, NZ * NC, *strip),
            vm((DIRECT, NX, COLBLK) + strip, BF16),
            per_chunk(DIRECT, NX, COLBLK, *strip),
            vm((NX, NC, NZ) + piece, BF16),
            vm((SLOTS, NZ) + piece, BF16),
            vm((NZ, SLOTS) + piece, BF16),
            vm((2, NX, COLBLK) + piece, BF16),
            vm((2, NX, COLBLK) + piece, BF16),
            vm((NX, COLBLK) + piece, BF16),
            vm((CHUNKS, NX, NC, HALF) + piece, BF16),
            vm((CHUNKS, SLOTS, HALF) + piece, BF16),
            per_chunk(CHUNKS, NZ, SLOTS, *piece),
            vm((CHUNKS, NX, COLBLK) + piece, BF16),
            vm((CHUNKS, NX, COLBLK) + piece, BF16),
            pltpu.SMEM((1, n_blocks), jnp.int32),
            vm((1, n_blocks), jnp.int32),
            vm((8, 128), jnp.int32),
            pltpu.SMEM((8, 128), jnp.int32),
            vm((1024, RC, LANE), BF16),
            dma((6,)),
            dma((4,)),
            dma((len(RECV),)),
        ],
        compiler_params=pltpu.CompilerParams(
            collective_id=0, has_side_effects=True, vmem_limit_bytes=59 * 2**20
        ),
        cost_estimate=pl.CostEstimate(
            flops=16 * BLOCK**3, bytes_accessed=12 * 2**20, transcendentals=BLOCK**2
        ),
    )(
        block_target,
        gradient,
        first_moment,
        left_gram[0, 0],
        right_gram[0, 0],
        left_basis[0, 0].reshape(HALF * NC, ROWS, BLOCK),
        right_basis[0, 0],
        second_moment[0, 0],
    )
    out = pl.pallas_call(
        write_out,
        out_shape=tuple(jax.ShapeDtypeStruct(s, d) for s, d in shapes),
        in_specs=[vmem_spec] * 5,
        out_specs=(any_spec,) * 5,
        scratch_shapes=[dma((5,))],
        compiler_params=pltpu.CompilerParams(vmem_limit_bytes=2**20),
    )(*held)
    return (out[0], out[1]) + tuple(o[None, None] for o in out[2:])


def solution(mesh):
    return jax.shard_map(
        shards,
        mesh=mesh,
        in_specs=(
            P("fsdp", "mp"),
            P("fsdp", "mp"),
            P("fsdp", "mp", None, None),
            P("fsdp", "mp", None, None),
            P("fsdp", "mp", None, None),
            P("fsdp", "mp", None, None),
            P("fsdp", "mp", None, None),
            P("mp", None),
        ),
        out_specs=(
            P("fsdp", "mp"),
            P("fsdp", "mp"),
            P("fsdp", "mp", None, None),
            P("fsdp", "mp", None, None),
            P("fsdp", "mp", None, None),
        ),
        check_vma=False,
    )
```
